256 devices in a mesh: seq: 16 (over x, z_hi, core), fsdp: 16 (over y, z_lo).
Axes of the slice: x: 4, y: 4, z: 8 (z_hi: 2, z_lo: 4; z = z_hi * 4 + z_lo), core: 2. Of those that a mesh axis runs over, the one named last changes fastest.
Arguments:
- queries: bfloat16 [16, 3, 2048, 1536], P('fsdp', None, 'seq'), as said below
- key_rows: bfloat16 [16, 3, 2048, 1536], P('fsdp', None, 'seq'), may hold values from -4 to 4
- value_rows: bfloat16 [16, 3, 2048, 1536], P('fsdp', None, 'seq'), may hold values from -6 to 6
- text_keys: bfloat16 [16, 256, 1536], P('fsdp', 'seq'), may hold values from -6 to 6
- text_values: bfloat16 [16, 256, 1536], P('fsdp', 'seq'), may hold values from -6 to 6
- residual: bfloat16 [16, 3, 2048, 3072], P('fsdp', None, 'seq'), may hold values from -4 to 4
- out_gate: float32 [3072], replicated, may hold values from -6 to 6
- out_weight: bfloat16 [1536, 3072], P(None, 'fsdp'), may hold values from -0.15625 to 0.15625
- out_bias: float32 [3072], replicated, may hold values from -2 to 2
- tile_lists: int32 [16, 3, 16, 27], P('fsdp', None, 'seq'), may hold values from -1 to 47, as said below
Outputs:
- mixed: bfloat16 [16, 3, 2048, 3072], P('fsdp', None, 'seq')
The draws below stay inside these ranges and needn't reach their ends.
Inputs may be any that keep to these rules, and one draw needn't show every extreme that they name: `tile_lists`: tile s of a clip lies at grid position (t, h, w) with s = (t * 8 + h) * 2 + w, 0 <= t < 3, 0 <= h < 8, 0 <= w < 2. The list of tile s names s itself and some of the other tiles of the same clip whose three grid coordinates each differ from those of s by at most one, each tile at most once, in any order, the remaining entries being -1. `queries`: entries lie within 8 or 240 / sqrt(128) in magnitude, whichever is larger.
All inputs are finite; a program needn't handle non-finite values.
Results may differ from the reference program's by a relative error of at most 0.0053.
Values may be sent and summed in bfloat16 or wider, within the bound.
No kernel may reach another device: no remote copies, remote signals or barrier semaphores. Data moves between devices by JAX's collectives and lax.ppermute only.
A program may use at most 192 MiB of HBM per device.

```python
import jax
import jax.numpy as jnp
from jax import lax

D = 3072
HEADS = 12
HD = 128
TILE = 128
TEXT = 256
KT = 27
GW = 2
GT = 3
HID = 1536
SPOTS = 16
GH = 8
TILES = 48
CLIPS = 16


def draw_key_rows(key, part):
    key = jax.random.fold_in(key, 1)
    return jax.random.truncated_normal(key, -4.0, 4.0, (CLIPS, GT, SPOTS * TILE, HID), jnp.float32).astype(jnp.bfloat16)


def draw_queries(key, part):
    key = jax.random.fold_in(key, 2)
    return (2.0 * jax.random.truncated_normal(key, -4.0, 4.0, (CLIPS, GT, SPOTS * TILE, HID), jnp.float32)).astype(jnp.bfloat16)


def draw_tile_lists(key, part):
    key = jax.random.fold_in(key, 3)
    slot_ids = jnp.arange(CLIPS * TILES, dtype=jnp.int32) % TILES
    time_pos = slot_ids // SPOTS
    height_pos = slot_ids % SPOTS // GW
    width_pos = slot_ids % GW
    columns = jnp.arange(KT, dtype=jnp.int32)
    time_step = columns // 9 - 1
    height_step = columns // 3 % 3 - 1
    width_step = columns % 3 - 1
    time_new = time_pos[:, None] + time_step[None, :]
    height_new = height_pos[:, None] + height_step[None, :]
    width_new = width_pos[:, None] + width_step[None, :]
    inside = (time_new >= 0) & (time_new < GT) & (height_new >= 0) & (height_new < GH) & (width_new >= 0) & (width_new < GW)
    target = (time_new * GH + height_new) * GW + width_new
    coin_flip = jax.random.randint(key, (CLIPS * TILES, KT), 0, 5)
    centre = (time_step == 0) & (height_step == 0) & (width_step == 0)
    keep_flags = inside & (centre[None, :] | (coin_flip < 3))
    rank_score = jnp.where(keep_flags, 0, KT) + columns[None, :]
    ordering = jnp.argsort(rank_score, axis=1)
    kept_flags = jnp.take_along_axis(keep_flags, ordering, axis=1)
    named_tiles = jnp.take_along_axis(target, ordering, axis=1)
    return jnp.where(kept_flags, named_tiles, -1).astype(jnp.int32).reshape(CLIPS, GT, SPOTS, KT)


def block_levels(stream_key, dims, shards, least, top_value):
    level, own = 1.0, jax.random.fold_in(stream_key, 6)
    for dim, parts in shards:
        steps = jnp.exp(jax.random.uniform(jax.random.fold_in(own, dim), (parts,), jnp.float32, least / len(shards), top_value / len(shards)))
        level = level * jnp.repeat(steps, dims[dim] // parts).reshape([-1 if axis == dim else 1 for axis in range(len(dims))])
    return level


def gaussian(rng, dims, width, bound, pieces=(), kind=jnp.bfloat16):
    values = jax.random.normal(rng, dims, jnp.float32) * width
    if len(pieces) > 0:
        values = block_levels(rng, dims, pieces, -0.22, 0.18) * values
    return jnp.clip(values, min=-bound, max=bound).astype(kind)


def setup_inputs(seed: int = 0) -> dict:
    key_of = jax.random.split(jax.random.key(seed), 11)
    return {
        "queries": draw_queries(jax.random.fold_in(key_of[10], 71), 0),
        "key_rows": draw_key_rows(jax.random.fold_in(key_of[10], 71), 0),
        "value_rows": gaussian(key_of[2], (CLIPS, GT, SPOTS * TILE, HID), 1.0, 6.0, ((0, 16), (2, 16))),
        "text_keys": gaussian(key_of[3], (CLIPS, TEXT, HID), 1.0, 6.0, ((0, 16), (1, 16))),
        "text_values": gaussian(key_of[4], (CLIPS, TEXT, HID), 1.0, 6.0, ((0, 16), (1, 16))),
        "residual": gaussian(key_of[5], (CLIPS, GT, SPOTS * TILE, D), 0.5, 4.0, ((0, 16), (2, 16))),
        "out_gate": gaussian(key_of[6], (D,), 1.5, 6.0, (), jnp.float32),
        "out_weight": gaussian(key_of[7], (HID, D), HID ** -0.5, 0.15625, ((1, 16),)),
        "out_bias": gaussian(key_of[8], (D,), 0.3, 2.0, (), jnp.float32),
        "tile_lists": draw_tile_lists(jax.random.fold_in(key_of[10], 71), 0),
    }


def reference(queries, key_rows, value_rows, text_keys, text_values, residual, out_gate, out_weight, out_bias, tile_lists):
    score_scale = HD ** -0.5
    key_tiles = key_rows.reshape(CLIPS, TILES, TILE, HEADS, HD)
    value_tiles = value_rows.reshape(CLIPS, TILES, TILE, HEADS, HD)
    query_tiles = queries.reshape(CLIPS * TILES, TILE, HEADS, HD)
    list_rows = tile_lists.reshape(CLIPS * TILES, KT)

    def one_tile(flat_index):
        clip_index = flat_index // TILES
        listed = list_rows[flat_index]
        chosen = jnp.maximum(listed, 0).astype(jnp.int32)
        clip_keys = key_tiles[clip_index]
        clip_values = value_tiles[clip_index]
        picked_keys = clip_keys[chosen].reshape(KT * TILE, HEADS, HD).astype(jnp.float32)
        picked_values = clip_values[chosen].reshape(KT * TILE, HEADS, HD).astype(jnp.float32)
        text_key_heads = text_keys[clip_index].reshape(TEXT, HEADS, HD).astype(jnp.float32)
        text_value_heads = text_values[clip_index].reshape(TEXT, HEADS, HD).astype(jnp.float32)
        allowed = jnp.repeat(listed >= 0, TILE)
        query_tile = query_tiles[flat_index].astype(jnp.float32)
        local_scores = jnp.einsum('qhd,khd->hqk', query_tile, picked_keys) * score_scale
        local_scores = jnp.where(allowed[None, None, :], local_scores, -jnp.inf)
        text_scores = jnp.einsum('qhd,khd->hqk', query_tile, text_key_heads) * score_scale
        scores = jnp.concatenate([local_scores, text_scores], axis=2)
        row_peak = jnp.max(scores, axis=2, keepdims=True)
        exponent = jnp.exp(scores - row_peak)
        weights = (exponent / jnp.sum(exponent, axis=2, keepdims=True)).astype(jnp.bfloat16)
        weights = lax.optimization_barrier(weights)
        all_values = jnp.concatenate([picked_values, text_value_heads], axis=0)
        combined = jnp.einsum('hqk,khd->qhd', weights.astype(jnp.float32), all_values)
        return combined.reshape(TILE, HEADS * HD).astype(jnp.bfloat16)

    attended = lax.map(one_tile, jnp.arange(CLIPS * TILES, dtype=jnp.int32)).reshape(CLIPS * TILES * TILE, HEADS * HD)
    projected = (jnp.dot(attended, out_weight, preferred_element_type=jnp.float32) + out_bias).astype(jnp.bfloat16)
    projected = lax.optimization_barrier(projected)
    projected = projected.reshape(residual.shape)
    return (residual.astype(jnp.float32) + out_gate * projected.astype(jnp.float32)).astype(jnp.bfloat16)
```

```python
import functools

import jax
import jax.numpy as jnp
from jax import lax
from jax.experimental import pallas as pl
from jax.experimental.pallas import tpu as pltpu
from jax.sharding import PartitionSpec as P

HEADS = 12
HD = 128
TILE = 128
GT = 3
ROWS = GT * TILE
HID = HEADS * HD
QUARTER = HID // 4
PANEL = 192
D = 3072
TEXT = 256
GROUPS = (3, 3, 3, 2, 1)
NEG = -1e30
SCALE = HD**-0.5 * 1.4426950408889634
AXES = ("seq", "fsdp")


def place(x, y, z, c):
    return (((x % 4) * 2 + z % 8 // 4) * 2 + c % 2) * 16 + (y % 4) * 4 + z % 4


def shift(value, dx=0, dy=0, dz=0, dc=0):
    pairs = [
        (place(x, y, z, c), place(x + dx, y + dy, z + dz, c + dc))
        for x in range(4)
        for y in range(4)
        for z in range(8)
        for c in range(2)
    ]
    return lax.ppermute(value, AXES, pairs)


def forward(value, flip=0):
    pairs = [(s, ((s + 4) % 16 if s % 4 < 2 else (s - 4) % 16) ^ flip) for s in range(16)]
    return lax.ppermute(value, "seq", pairs)


def after(value, *earlier):
    return lax.optimization_barrier((value, earlier))[0]


def attend_kernel(bias, q, k0, v0, k1, v1, b0, b1, c0, c1, tk, tv, out):
    contract = (((1,), (1,)), ((), ()))
    sources = [(k0, v0), (k1, v1)] + [(r.at[0], r.at[1]) for r in (b0, b1, c0, c1)]
    for t in range(GT):
        low, high = max(0, t - 1), min(GT, t + 2)
        qt = q[t * TILE : (t + 1) * TILE, :]
        pieces = []
        peak = None
        for n, (k, _) in enumerate(sources):
            s = lax.dot_general(
                qt, k[low * TILE : high * TILE, :], contract, preferred_element_type=jnp.float32
            )
            for j in range(low, high):
                part = s[:, (j - low) * TILE : (j - low + 1) * TILE] * SCALE + bias[t, n * GT + j]
                pieces.append(part)
                peak = part if peak is None else jnp.maximum(peak, part)
        s = lax.dot_general(qt, tk[...], contract, preferred_element_type=jnp.float32) * SCALE
        for j in range(TEXT // TILE):
            part = s[:, j * TILE : (j + 1) * TILE]
            pieces.append(part)
            peak = jnp.maximum(peak, part)
        top = jnp.max(peak, axis=1, keepdims=True)
        total = jnp.zeros((TILE, TILE), jnp.float32)
        acc = jnp.zeros((TILE, HD), jnp.float32)
        at = 0
        for n in range(len(sources) + 1):
            if n < len(sources):
                count = high - low
                values = sources[n][1][low * TILE : high * TILE, :]
            else:
                count = TEXT // TILE
                values = tv[...]
            weights = []
            for j in range(count):
                e = jnp.exp2(pieces[at + j] - top)
                total = total + e
                weights.append(e.astype(jnp.bfloat16))
            at += count
            acc = acc + jnp.dot(
                jnp.concatenate(weights, axis=1), values, preferred_element_type=jnp.float32
            )
        row = jnp.sum(total, axis=1, keepdims=True)
        out[t * TILE : (t + 1) * TILE, :] = (acc / row).astype(jnp.bfloat16)


def attend(bias, q, k0, v0, k1, v1, near, far, tk, tv, first, count):
    wide = pl.BlockSpec((ROWS, HD), lambda i: (0, first + i))
    text = pl.BlockSpec((TEXT, HD), lambda i: (0, first + i))
    pack = pl.BlockSpec((2, ROWS, HD), lambda i: (0, 0, i))
    units = 48 * count
    return pl.pallas_call(
        attend_kernel,
        grid=(count,),
        out_shape=jax.ShapeDtypeStruct((ROWS, count * HD), jnp.bfloat16),
        in_specs=[pl.BlockSpec(memory_space=pltpu.SMEM)]
        + [wide] * 5
        + [pack] * 4
        + [text] * 2,
        out_specs=pl.BlockSpec((ROWS, HD), lambda i: (0, i)),
        compiler_params=pltpu.CompilerParams(vmem_limit_bytes=24 * 1024 * 1024),
        cost_estimate=pl.CostEstimate(
            flops=units * TILE * TILE * HD * 16,
            bytes_accessed=count * 2 * HD * (ROWS * 14 + TEXT * 2),
            transcendentals=units * TILE * TILE,
        ),
        name="attend",
    )(bias, q, k0, v0, k1, v1, *near, *far, tk, tv)


def project_kernel(*refs):
    parts = refs[: len(GROUPS)]
    order, wa, wb, wc_low, wc_high, wd_low, wd_high, bias, gate, residual, out, att, mine = refs[
        len(GROUPS) :
    ]
    step = pl.program_id(0)

    @pl.when(step == 0)
    def _():
        head = 0
        for part in parts:
            for n in range(part.shape[1] // HD):
                column = head % 3 * HD
                att[head // 3, :, column : column + HD] = part[:, n * HD : (n + 1) * HD]
                head += 1
        for n in range(4):
            mine[:, n * QUARTER : (n + 1) * QUARTER] = att[order[n]]

    low = step < pl.num_programs(0) // 2
    wt = jnp.concatenate(
        [
            wa[...],
            wb[...],
            jnp.where(low, wc_low[...], wc_high[...]),
            jnp.where(low, wd_low[...], wd_high[...]),
        ],
        axis=1,
    )
    projected = lax.dot_general(
        mine[...], wt, (((1,), (1,)), ((), ())), preferred_element_type=jnp.float32
    )
    projected = (projected + bias[...]).astype(jnp.bfloat16).astype(jnp.float32)
    out[...] = (residual[...].astype(jnp.float32) + gate[...] * projected).astype(jnp.bfloat16)


def project(parts, order, weights, bias, gate, residual):
    step = 512
    half = D // step // 2
    whole = pl.BlockSpec((step, QUARTER), lambda i: (i, 0))
    low = pl.BlockSpec((step, QUARTER), lambda i: (jnp.minimum(i, half - 1), 0))
    high = pl.BlockSpec((step, QUARTER), lambda i: (jnp.maximum(i - half, 0), 0))
    return pl.pallas_call(
        project_kernel,
        grid=(D // step,),
        out_shape=jax.ShapeDtypeStruct((ROWS, D), jnp.bfloat16),
        in_specs=[pl.BlockSpec(part.shape, lambda i: (0, 0)) for part in parts]
        + [pl.BlockSpec(memory_space=pltpu.SMEM)]
        + [whole, whole, low, high, low, high]
        + [
            pl.BlockSpec((1, step), lambda i: (0, i)),
            pl.BlockSpec((1, step), lambda i: (0, i)),
            pl.BlockSpec((ROWS, step), lambda i: (0, i)),
        ],
        out_specs=pl.BlockSpec((ROWS, step), lambda i: (0, i)),
        scratch_shapes=[
            pltpu.VMEM((4, ROWS, QUARTER), jnp.bfloat16),
            pltpu.VMEM((ROWS, HID), jnp.bfloat16),
        ],
        compiler_params=pltpu.CompilerParams(vmem_limit_bytes=32 * 1024 * 1024),
        cost_estimate=pl.CostEstimate(
            flops=2 * ROWS * HID * D,
            bytes_accessed=2 * D * HID + 4 * ROWS * D,
            transcendentals=0,
        ),
        name="project",
    )(*parts, order, *weights, bias, gate, residual)


def place_all(own, index, others):
    whole = jnp.zeros((4,) + own.shape, own.dtype)
    for piece, at in [(own, index)] + others:
        whole = lax.dynamic_update_index_in_dim(whole, piece, at % 4, 0)
    return whole


def local(
    queries,
    key_rows,
    value_rows,
    text_keys,
    text_values,
    residual,
    out_gate,
    out_weight,
    out_bias,
    tile_lists,
):
    seq, fsdp = lax.axis_index("seq"), lax.axis_index("fsdp")
    x, zh, c = seq // 4, seq // 2 % 2, seq % 2
    y, zl = fsdp // 4, fsdp % 4
    q = queries.reshape(ROWS, HID)
    k0, v0 = key_rows.reshape(ROWS, HID), value_rows.reshape(ROWS, HID)

    packs = []
    first = 0
    for count in GROUPS:
        columns = slice(first * HD, (first + count) * HD)
        packs.append(jnp.stack([k0[:, columns], v0[:, columns]]))
        first += count

    text = jnp.concatenate([text_keys, text_values], axis=0)
    text = jnp.concatenate([text, shift(text, dz=4)], axis=1)
    piece = lax.dynamic_slice(
        out_weight.T, (0, (x % 2 * 2 + c) * QUARTER), (PANEL, QUARTER)
    )
    wz = place_all(piece, zl, [(shift(piece, dz=d), zl - d) for d in (1, -1, 2)])
    k1, v1 = shift(k0, dc=1), shift(v0, dc=1)

    text = jnp.concatenate([text] + [shift(text, dx=d) for d in (1, -1, 2)], axis=1)
    wy = place_all(wz, y, [(shift(wz, dy=d), y - d) for d in (1, -1, 2)])
    text_more = shift(text, dc=1)
    text = jnp.concatenate([text, text_more], axis=1)

    last = len(GROUPS) - 1
    far_spot = jnp.where(zh == 0, seq - 2, seq + 2)
    spots = jnp.stack(
        [seq, seq ^ 1, seq ^ 2, seq ^ 3, far_spot, far_spot ^ 1]
    )
    inside = (spots >= 0) & (spots < 16)
    candidates = spots[:, None] + 16 * jnp.arange(GT, dtype=jnp.int32)[None, :]
    listed = tile_lists[0, :, 0, :]
    present = jnp.any(listed[:, None, None, :] == candidates[None, :, :, None], axis=3)
    present = present & inside[None, :, None]
    bias = jnp.where(present, 0.0, NEG).astype(jnp.float32).reshape(GT, 6 * GT)

    near = [shift(packs[0], dz=4), shift(packs[1], dz=4)]
    parts = []
    first = 0
    for g, count in enumerate(GROUPS):
        if g > 0:
            near[g] = after(near[g], far, near_other)
        near_other = shift(near[g], dc=1)
        far = forward(near[g])
        if g < last:
            far_other = shift(far, dc=1)
        else:
            far_other = forward(near[g], flip=1)
        if g + 2 <= last:
            waits = (far, near_other) + tuple(parts[g - 1 :])
            if g == 0:
                waits += (text_more,)
                wx_low = shift(after(wy[:2], near[0]), dx=1)
                wx_high = shift(after(wy[2:], near[0]), dx=-1)
            if g == 1:
                waits += (wx_low, wx_high)
                wb = shift(after(wy, near[1]), dc=1)
            if g == 2:
                waits += (wb,)
                wd_low, wd_high = shift(wx_low, dc=1), shift(wx_high, dc=1)
            near.append(shift(after(packs[g + 2], *waits), dz=4))
        parts.append(
            attend(
                bias,
                q,
                k0,
                v0,
                k1,
                v1,
                (near[g], near_other),
                (far, far_other),
                text[0],
                text[1],
                first,
                count,
            )
        )
        first += count
    own = x % 2 * 2 + c
    order = jnp.stack([own, own ^ 1, own ^ 2, own ^ 3]).astype(jnp.int32)
    weights = [w.reshape(-1, QUARTER) for w in (wy, wb, wx_low, wx_high, wd_low, wd_high)]
    mixed = project(
        parts,
        order,
        weights,
        out_bias.reshape(1, D),
        out_gate.reshape(1, D),
        residual.reshape(ROWS, D),
    )
    return mixed.reshape(residual.shape)


def solution(mesh):
    placed = (
        P("fsdp", None, "seq", None),
        P("fsdp", None, "seq", None),
        P("fsdp", None, "seq", None),
        P("fsdp", "seq", None),
        P("fsdp", "seq", None),
        P("fsdp", None, "seq", None),
        P(),
        P(None, "fsdp"),
        P(),
        P("fsdp", None, "seq", None),
    )
    return jax.shard_map(
        local, mesh=mesh, in_specs=placed, out_specs=P("fsdp", None, "seq", None), check_vma=False
    )
```

```python
import functools

import jax
import jax.numpy as jnp
from jax import lax
from jax.experimental import pallas as pl
from jax.experimental.pallas import tpu as pltpu
from jax.sharding import PartitionSpec as P

HEADS = 12
HD = 128
TILE = 128
GT = 3
ROWS = GT * TILE
HID = HEADS * HD
QUARTER = HID // 4
PANEL = 192
D = 3072
TEXT = 256
GROUPS = (5, 4, 2, 1)
NEG = -1e30
SCALE = HD**-0.5 * 1.4426950408889634
AXES = ("seq", "fsdp")


def place(x, y, z, c):
    return (((x % 4) * 2 + z % 8 // 4) * 2 + c % 2) * 16 + (y % 4) * 4 + z % 4


def shift(value, dx=0, dy=0, dz=0, dc=0):
    pairs = [
        (place(x, y, z, c), place(x + dx, y + dy, z + dz, c + dc))
        for x in range(4)
        for y in range(4)
        for z in range(8)
        for c in range(2)
    ]
    return lax.ppermute(value, AXES, pairs)


def forward(value, flip=0):
    pairs = [(s, ((s + 4) % 16 if s % 4 < 2 else (s - 4) % 16) ^ flip) for s in range(16)]
    return lax.ppermute(value, "seq", pairs)


def swap(value, bit):
    return lax.ppermute(value, "seq", [(s, s ^ bit) for s in range(16)])


def across(value):
    pairs = [(s, (s - 4) % 16 if s % 4 < 2 else (s + 4) % 16) for s in range(16)]
    return lax.ppermute(value, "seq", pairs)


def join_kernel(*refs):
    first = 0
    for ref in refs[:-1]:
        refs[-1][:, first : first + ref.shape[1], :] = ref[...]
        first += ref.shape[1]


def join(*pieces):
    rows = sum(p.shape[1] for p in pieces)
    return pl.pallas_call(
        join_kernel,
        out_shape=jax.ShapeDtypeStruct((2, rows, HID), jnp.bfloat16),
        compiler_params=pltpu.CompilerParams(vmem_limit_bytes=16 * 1024 * 1024),
        cost_estimate=pl.CostEstimate(
            flops=0, bytes_accessed=8 * rows * HID, transcendentals=0
        ),
        name="join",
    )(*pieces)


def merge_kernel(near, far, out):
    out[:2] = near[...]
    out[2:] = far[...]


def merge(near, far):
    return pl.pallas_call(
        merge_kernel,
        grid=(near.shape[2] // HD,),
        out_shape=jax.ShapeDtypeStruct((4,) + near.shape[1:], jnp.bfloat16),
        in_specs=[pl.BlockSpec((2, ROWS, HD), lambda i: (0, 0, i))] * 2,
        out_specs=pl.BlockSpec((4, ROWS, HD), lambda i: (0, 0, i)),
        cost_estimate=pl.CostEstimate(flops=0, bytes_accessed=8 * near.size, transcendentals=0),
        name="merge",
    )(near, far)


def pair_kernel(k, v, out):
    out[0] = k[...]
    out[1] = v[...]


def pair(k, v, first, count, width=HD):
    rows = k.shape[0]
    return pl.pallas_call(
        pair_kernel,
        grid=(count,),
        out_shape=jax.ShapeDtypeStruct((2, rows, count * width), jnp.bfloat16),
        in_specs=[pl.BlockSpec((rows, width), lambda i: (0, first + i))] * 2,
        out_specs=pl.BlockSpec((2, rows, width), lambda i: (0, 0, i)),
        compiler_params=pltpu.CompilerParams(vmem_limit_bytes=16 * 1024 * 1024),
        cost_estimate=pl.CostEstimate(
            flops=0, bytes_accessed=8 * rows * count * width, transcendentals=0
        ),
        name="pair",
    )(k, v)


def place_kernel(where, *refs):
    for n, ref in enumerate(refs[:-1]):
        refs[-1][where[n]] = ref[...]


def place_all(where, *pieces):
    shape = (4,) + pieces[0].shape
    size = 4 * pieces[0].size
    return pl.pallas_call(
        place_kernel,
        out_shape=jax.ShapeDtypeStruct(shape, jnp.bfloat16),
        in_specs=[pl.BlockSpec(memory_space=pltpu.SMEM)]
        + [pl.BlockSpec(memory_space=pltpu.VMEM)] * 4,
        compiler_params=pltpu.CompilerParams(vmem_limit_bytes=16 * 1024 * 1024),
        cost_estimate=pl.CostEstimate(flops=0, bytes_accessed=4 * size, transcendentals=0),
        name="place",
    )(where, *pieces)


def attend_kernel(bias, q, k0, v0, a1, b0, b1, c0, c1, words, out):
    contract = (((1,), (1,)), ((), ()))
    sources = [(k0, v0)] + [(r.at[0], r.at[1]) for r in (a1, b0, b1, c0, c1)]
    for t in range(GT):
        low, high = max(0, t - 1), min(GT, t + 2)
        qt = q[t * TILE : (t + 1) * TILE, :]
        pieces = []
        peak = None
        for n, (k, _) in enumerate(sources):
            s = lax.dot_general(
                qt, k[low * TILE : high * TILE, :], contract, preferred_element_type=jnp.float32
            )
            for j in range(low, high):
                part = s[:, (j - low) * TILE : (j - low + 1) * TILE] * SCALE + bias[t, n * GT + j]
                pieces.append(part)
                peak = part if peak is None else jnp.maximum(peak, part)
        s = lax.dot_general(qt, words[0], contract, preferred_element_type=jnp.float32) * SCALE
        for j in range(TEXT // TILE):
            part = s[:, j * TILE : (j + 1) * TILE]
            pieces.append(part)
            peak = jnp.maximum(peak, part)
        top = jnp.max(peak, axis=1, keepdims=True)
        total = jnp.zeros((TILE, TILE), jnp.float32)
        acc = jnp.zeros((TILE, HD), jnp.float32)
        at = 0
        for n in range(len(sources) + 1):
            if n < len(sources):
                count = high - low
                values = sources[n][1][low * TILE : high * TILE, :]
            else:
                count = TEXT // TILE
                values = words[1]
            weights = []
            for j in range(count):
                e = jnp.exp2(pieces[at + j] - top)
                total = total + e
                weights.append(e.astype(jnp.bfloat16))
            at += count
            acc = acc + jnp.dot(
                jnp.concatenate(weights, axis=1), values, preferred_element_type=jnp.float32
            )
        row = jnp.sum(total, axis=1, keepdims=True)
        out[t * TILE : (t + 1) * TILE, :] = (acc / row).astype(jnp.bfloat16)


def attend(bias, q, k0, v0, beside, near, far, text, first, count, merged=False):
    wide = pl.BlockSpec((ROWS, HD), lambda i: (0, first + i))
    words = pl.BlockSpec((2, TEXT, HD), lambda i: (0, 0, first + i))
    pack = pl.BlockSpec((2, ROWS, HD), lambda i: (0, 0, i))
    upper = pl.BlockSpec((2, ROWS, HD), lambda i: (1, 0, i))
    whole = pl.BlockSpec((2, ROWS, HD), lambda i: (0, 0, first + i))
    units = 48 * count
    return pl.pallas_call(
        attend_kernel,
        grid=(count,),
        out_shape=jax.ShapeDtypeStruct((ROWS, count * HD), jnp.bfloat16),
        in_specs=[pl.BlockSpec(memory_space=pltpu.SMEM)]
        + [wide] * 3
        + [whole]
        + [pack] * 3
        + [upper if merged else pack]
        + [words],
        out_specs=pl.BlockSpec((ROWS, HD), lambda i: (0, i)),
        compiler_params=pltpu.CompilerParams(vmem_limit_bytes=14 * 1024 * 1024),
        cost_estimate=pl.CostEstimate(
            flops=units * TILE * TILE * HD * 16,
            bytes_accessed=count * 2 * HD * (ROWS * 14 + TEXT * 2),
            transcendentals=units * TILE * TILE,
        ),
        name="attend",
    )(bias, q, k0, v0, beside, *near, *far, text)


def project_kernel(*refs):
    parts = refs[: len(GROUPS)]
    order, wa, wb, wc, wd, bias, gate, residual, out, att, mine = refs[
        len(GROUPS) :
    ]
    step = pl.program_id(0)

    @pl.when(step == 0)
    def _():
        head = 0
        for part in parts:
            for n in range(part.shape[1] // HD):
                column = head % 3 * HD
                att[head // 3, :, column : column + HD] = part[:, n * HD : (n + 1) * HD]
                head += 1
        for n in range(4):
            mine[:, n * QUARTER : (n + 1) * QUARTER] = att[order[n]]

    wt = jnp.concatenate([wa[...], wb[...], wc[...], wd[...]], axis=1)
    projected = lax.dot_general(
        mine[...], wt, (((1,), (1,)), ((), ())), preferred_element_type=jnp.float32
    )
    projected = (projected + bias[...]).astype(jnp.bfloat16).astype(jnp.float32)
    out[...] = (residual[...].astype(jnp.float32) + gate[...] * projected).astype(jnp.bfloat16)


def project(parts, order, weights, bias, gate, residual):
    step = 512
    panel = pl.BlockSpec((step, QUARTER), lambda i: (i, 0))
    return pl.pallas_call(
        project_kernel,
        grid=(D // step,),
        out_shape=jax.ShapeDtypeStruct((ROWS, D), jnp.bfloat16),
        in_specs=[pl.BlockSpec(part.shape, lambda i: (0, 0)) for part in parts]
        + [pl.BlockSpec(memory_space=pltpu.SMEM)]
        + [panel] * 4
        + [
            pl.BlockSpec((1, step), lambda i: (0, i)),
            pl.BlockSpec((1, step), lambda i: (0, i)),
            pl.BlockSpec((ROWS, step), lambda i: (0, i)),
        ],
        out_specs=pl.BlockSpec((ROWS, step), lambda i: (0, i)),
        scratch_shapes=[
            pltpu.VMEM((4, ROWS, QUARTER), jnp.bfloat16),
            pltpu.VMEM((ROWS, HID), jnp.bfloat16),
        ],
        compiler_params=pltpu.CompilerParams(vmem_limit_bytes=14 * 1024 * 1024),
        cost_estimate=pl.CostEstimate(
            flops=2 * ROWS * HID * D,
            bytes_accessed=2 * D * HID + 4 * ROWS * D,
            transcendentals=0,
        ),
        name="project",
    )(*parts, order, *weights, bias, gate, residual)


def stage(ready, work, *operands):
    shapes = jax.eval_shape(work, *operands)
    return lax.cond(
        ready,
        work,
        lambda *_: tuple(jnp.zeros(s.shape, s.dtype) for s in shapes),
        *operands,
    )


def local(
    queries,
    key_rows,
    value_rows,
    text_keys,
    text_values,
    residual,
    out_gate,
    out_weight,
    out_bias,
    tile_lists,
):
    seq, fsdp = lax.axis_index("seq"), lax.axis_index("fsdp")
    x, zh, c = seq // 4, seq // 2 % 2, seq % 2
    y, zl = fsdp // 4, fsdp % 4
    q = queries.reshape(ROWS, HID)
    k0, v0 = key_rows.reshape(ROWS, HID), value_rows.reshape(ROWS, HID)

    far_spot = jnp.where(zh == 0, seq - 2, seq + 2)
    spots = jnp.stack(
        [seq, seq ^ 1, seq ^ 2, seq ^ 3, far_spot, far_spot ^ 1]
    )
    inside = (spots >= 0) & (spots < 16)
    candidates = spots[:, None] + 16 * jnp.arange(GT, dtype=jnp.int32)[None, :]
    listed = tile_lists[0, :, 0, :]
    present = jnp.any(listed[:, None, None, :] == candidates[None, :, :, None], axis=3)
    present = present & inside[None, :, None]
    bias = jnp.where(present, 0.0, NEG).astype(jnp.float32).reshape(GT, 6 * GT)

    steps = jnp.array([0, 1, -1, 2], jnp.int32)
    firsts = [sum(GROUPS[:g]) for g in range(len(GROUPS))]
    packs = [pair(k0, v0, first, count) for first, count in zip(firsts, GROUPS)]

    def attend_group(g, near, others, far, text, far_other=None):
        return attend(
            bias,
            q,
            k0,
            v0,
            beside,
            (near, others),
            (far, others if far_other is None else far_other),
            text,
            firsts[g],
            GROUPS[g],
            far_other is None,
        )

    text = pair(text_keys[0], text_values[0], 0, 1, HID)
    piece = lax.dynamic_slice(
        out_weight.T, (0, (x % 2 * 2 + c) * QUARTER), (PANEL, QUARTER)
    )
    text_z = swap(text, 2)
    pack0, keys, values, wz1, wz2, wz3, text_z = lax.optimization_barrier(
        (
            packs[0],
            k0,
            v0,
            shift(piece, dz=1),
            shift(piece, dz=-1),
            shift(piece, dz=2),
            text_z,
        )
    )
    text = join(text, text_z)
    packs, bias, beside, wz1, wz2, wz3, text_x = lax.optimization_barrier(
        (
            packs[1:],
            bias,
            shift(pair(keys, values, 0, HEADS), dc=1),
            wz1,
            wz2,
            wz3,
            swap(text, 4),
        )
    )
    near0 = shift(pack0, dz=4)
    packs = (pack0,) + tuple(packs)
    ready = tile_lists[0, 0, 0, 0] > -2

    def weight_stage(piece, wz1, wz2, wz3, text, text_x):
        text = join(text, text_x)
        text = join(text, swap(text, 8))
        text = join(text, swap(text, 1))
        wz = place_all((zl - steps) % 4, piece, wz1, wz2, wz3)
        wy = place_all(
            (y - steps) % 4, wz, shift(wz, dy=1), shift(wz, dy=-1), shift(wz, dy=2)
        )
        return wy.reshape(D, QUARTER), text

    wy, text = stage(ready, weight_stage, piece, wz1, wz2, wz3, text, text_x)
    pack1, wy = lax.optimization_barrier((packs[1], wy))
    near1 = shift(pack1, dz=4)
    near0, wy = lax.optimization_barrier((near0, wy))
    wx = across(wy)

    def first_stage(near0):
        far0 = forward(near0)
        return far0, shift(near0, dc=1), shift(far0, dc=1)

    far0, near0_other, far0_other = stage(ready, first_stage, near0)

    def second_stage(near1, near0, near0_other, far0, far0_other, text):
        part0 = attend_group(0, near0, near0_other, far0, text, far0_other)
        near1_other = shift(near1, dc=1)
        far1, part0 = lax.optimization_barrier((forward(near1), part0))
        return part0, far1, near1_other, shift(far1, dc=1)

    pack2, near1, far0_other = lax.optimization_barrier((packs[2], near1, far0_other))
    near2 = shift(pack2, dz=4)
    part0, far1, near1_other, far1_other = stage(
        ready, second_stage, near1, near0, near0_other, far0, far0_other, text
    )

    def third_stage(near2, near1, near1_other, far1, far1_other, text, wy, wx):
        part1 = attend_group(1, near1, near1_other, far1, text, far1_other)
        wb, wd = shift(wy, dc=1), shift(wx, dc=1)
        far2, part1 = lax.optimization_barrier((forward(near2), part1))
        return part1, far2, shift(merge(near2, far2), dc=1), wb, wd

    pack3, near2, part0, wx = lax.optimization_barrier((packs[3], near2, part0, wx))
    near3 = shift(pack3, dz=4)
    part1, far2, others2, wb, wd = stage(
        ready,
        third_stage,
        near2,
        near1,
        near1_other,
        far1,
        far1_other,
        text,
        wy,
        wx,
    )
    near3, others2 = lax.optimization_barrier((near3, others2))
    part2 = attend_group(2, near2, others2, far2, text)
    far3, far3_other, near3_other, part2 = lax.optimization_barrier(
        (forward(near3), forward(near3, flip=1), shift(near3, dc=1), part2)
    )
    part3 = attend_group(3, near3, near3_other, far3, text, far3_other)
    parts = [part0, part1, part2, part3]
    own = x % 2 * 2 + c
    order = jnp.stack([own, own ^ 1, own ^ 2, own ^ 3]).astype(jnp.int32)
    weights = [w.reshape(-1, QUARTER) for w in (wy, wb, wx, wd)]
    mixed = project(
        parts,
        order,
        weights,
        out_bias.reshape(1, D),
        out_gate.reshape(1, D),
        residual.reshape(ROWS, D),
    )
    return mixed.reshape(residual.shape)


def solution(mesh):
    placed = (
        P("fsdp", None, "seq", None),
        P("fsdp", None, "seq", None),
        P("fsdp", None, "seq", None),
        P("fsdp", "seq", None),
        P("fsdp", "seq", None),
        P("fsdp", None, "seq", None),
        P(),
        P(None, "fsdp"),
        P(),
        P("fsdp", None, "seq", None),
    )
    return jax.shard_map(
        local, mesh=mesh, in_specs=placed, out_specs=P("fsdp", None, "seq", None), check_vma=False
    )
```

```python
import functools

import jax
import jax.numpy as jnp
from jax import lax
from jax.experimental import pallas as pl
from jax.experimental.pallas import tpu as pltpu
from jax.sharding import PartitionSpec as P

HEADS = 12
HD = 128
TILE = 128
GT = 3
ROWS = GT * TILE
HID = HEADS * HD
QUARTER = HID // 4
PANEL = 192
D = 3072
TEXT = 256
GROUPS = (4, 4, 3, 1)
NEG = -1e30
SCALE = HD**-0.5 * 1.4426950408889634
AXES = ("seq", "fsdp")


def place(x, y, z, c):
    return (((x % 4) * 2 + z % 8 // 4) * 2 + c % 2) * 16 + (y % 4) * 4 + z % 4


def shift(value, dx=0, dy=0, dz=0, dc=0):
    pairs = [
        (place(x, y, z, c), place(x + dx, y + dy, z + dz, c + dc))
        for x in range(4)
        for y in range(4)
        for z in range(8)
        for c in range(2)
    ]
    return lax.ppermute(value, AXES, pairs)


def forward(value, flip=0):
    pairs = [(s, ((s + 4) % 16 if s % 4 < 2 else (s - 4) % 16) ^ flip) for s in range(16)]
    return lax.ppermute(value, "seq", pairs)


def swap(value, bit):
    return lax.ppermute(value, "seq", [(s, s ^ bit) for s in range(16)])


def across(value):
    pairs = [(s, (s - 4) % 16 if s % 4 < 2 else (s + 4) % 16) for s in range(16)]
    return lax.ppermute(value, "seq", pairs)


def join_kernel(*refs):
    first = 0
    for ref in refs[:-1]:
        refs[-1][:, first : first + ref.shape[1], :] = ref[...]
        first += ref.shape[1]


def join(*pieces):
    rows = sum(p.shape[1] for p in pieces)
    return pl.pallas_call(
        join_kernel,
        out_shape=jax.ShapeDtypeStruct((2, rows, HID), jnp.bfloat16),
        compiler_params=pltpu.CompilerParams(vmem_limit_bytes=16 * 1024 * 1024),
        cost_estimate=pl.CostEstimate(
            flops=0, bytes_accessed=8 * rows * HID, transcendentals=0
        ),
        name="join",
    )(*pieces)


def merge_kernel(near, far, out):
    out[:2] = near[...]
    out[2:] = far[...]


def merge(near, far):
    return pl.pallas_call(
        merge_kernel,
        grid=(near.shape[2] // HD,),
        out_shape=jax.ShapeDtypeStruct((4,) + near.shape[1:], jnp.bfloat16),
        in_specs=[pl.BlockSpec((2, ROWS, HD), lambda i: (0, 0, i))] * 2,
        out_specs=pl.BlockSpec((4, ROWS, HD), lambda i: (0, 0, i)),
        cost_estimate=pl.CostEstimate(flops=0, bytes_accessed=8 * near.size, transcendentals=0),
        name="merge",
    )(near, far)


def pair_kernel(k, v, out):
    out[0] = k[...]
    out[1] = v[...]


def pair(k, v, first, count, width=HD):
    rows = k.shape[0]
    return pl.pallas_call(
        pair_kernel,
        grid=(count,),
        out_shape=jax.ShapeDtypeStruct((2, rows, count * width), jnp.bfloat16),
        in_specs=[pl.BlockSpec((rows, width), lambda i: (0, first + i))] * 2,
        out_specs=pl.BlockSpec((2, rows, width), lambda i: (0, 0, i)),
        compiler_params=pltpu.CompilerParams(vmem_limit_bytes=16 * 1024 * 1024),
        cost_estimate=pl.CostEstimate(
            flops=0, bytes_accessed=8 * rows * count * width, transcendentals=0
        ),
        name="pair",
    )(k, v)


def place_kernel(where, *refs):
    for n, ref in enumerate(refs[:-1]):
        refs[-1][where[n]] = ref[...]


def place_all(where, *pieces):
    shape = (4,) + pieces[0].shape
    size = 4 * pieces[0].size
    return pl.pallas_call(
        place_kernel,
        out_shape=jax.ShapeDtypeStruct(shape, jnp.bfloat16),
        in_specs=[pl.BlockSpec(memory_space=pltpu.SMEM)]
        + [pl.BlockSpec(memory_space=pltpu.VMEM)] * 4,
        compiler_params=pltpu.CompilerParams(vmem_limit_bytes=16 * 1024 * 1024),
        cost_estimate=pl.CostEstimate(flops=0, bytes_accessed=4 * size, transcendentals=0),
        name="place",
    )(where, *pieces)


def attend_kernel(bias, q, k0, v0, a1, b0, b1, c0, c1, words, out):
    contract = (((1,), (1,)), ((), ()))
    sources = [(k0, v0)] + [(r.at[0], r.at[1]) for r in (a1, b0, b1, c0, c1)]
    for t in range(GT):
        low, high = max(0, t - 1), min(GT, t + 2)
        qt = q[t * TILE : (t + 1) * TILE, :]
        pieces = []
        peak = None
        for n, (k, _) in enumerate(sources):
            s = lax.dot_general(
                qt, k[low * TILE : high * TILE, :], contract, preferred_element_type=jnp.float32
            )
            for j in range(low, high):
                part = s[:, (j - low) * TILE : (j - low + 1) * TILE] * SCALE + bias[t, n * GT + j]
                pieces.append(part)
                peak = part if peak is None else jnp.maximum(peak, part)
        s = lax.dot_general(qt, words[0], contract, preferred_element_type=jnp.float32) * SCALE
        for j in range(TEXT // TILE):
            part = s[:, j * TILE : (j + 1) * TILE]
            pieces.append(part)
            peak = jnp.maximum(peak, part)
        top = jnp.max(peak, axis=1, keepdims=True)
        total = jnp.zeros((TILE, TILE), jnp.float32)
        acc = jnp.zeros((TILE, HD), jnp.float32)
        at = 0
        for n in range(len(sources) + 1):
            if n < len(sources):
                count = high - low
                values = sources[n][1][low * TILE : high * TILE, :]
            else:
                count = TEXT // TILE
                values = words[1]
            weights = []
            for j in range(count):
                e = jnp.exp2(pieces[at + j] - top)
                total = total + e
                weights.append(e.astype(jnp.bfloat16))
            at += count
            acc = acc + jnp.dot(
                jnp.concatenate(weights, axis=1), values, preferred_element_type=jnp.float32
            )
        row = jnp.sum(total, axis=1, keepdims=True)
        out[t * TILE : (t + 1) * TILE, :] = (acc / row).astype(jnp.bfloat16)


def attend(bias, q, k0, v0, beside, near, far, text, first, count, merged=False):
    wide = pl.BlockSpec((ROWS, HD), lambda i: (0, first + i))
    words = pl.BlockSpec((2, TEXT, HD), lambda i: (0, 0, first + i))
    pack = pl.BlockSpec((2, ROWS, HD), lambda i: (0, 0, i))
    upper = pl.BlockSpec((2, ROWS, HD), lambda i: (1, 0, i))
    whole = pl.BlockSpec((2, ROWS, HD), lambda i: (0, 0, first + i))
    units = 48 * count
    return pl.pallas_call(
        attend_kernel,
        grid=(count,),
        out_shape=jax.ShapeDtypeStruct((ROWS, count * HD), jnp.bfloat16),
        in_specs=[pl.BlockSpec(memory_space=pltpu.SMEM)]
        + [wide] * 3
        + [whole]
        + [pack] * 3
        + [upper if merged else pack]
        + [words],
        out_specs=pl.BlockSpec((ROWS, HD), lambda i: (0, i)),
        compiler_params=pltpu.CompilerParams(vmem_limit_bytes=14 * 1024 * 1024),
        cost_estimate=pl.CostEstimate(
            flops=units * TILE * TILE * HD * 16,
            bytes_accessed=count * 2 * HD * (ROWS * 14 + TEXT * 2),
            transcendentals=units * TILE * TILE,
        ),
        name="attend",
    )(bias, q, k0, v0, beside, *near, *far, text)


def project_kernel(*refs):
    parts = refs[: len(GROUPS)]
    order, wa, wb, wc, wd, bias, gate, residual, out, mine = refs[
        len(GROUPS) :
    ]
    step = pl.program_id(0)

    @pl.when(step == 0)
    def _():
        head = 0
        for part in parts:
            for n in range(part.shape[1] // HD):
                column = pl.multiple_of(order[head // 3] * QUARTER + head % 3 * HD, HD)
                mine[:, pl.ds(column, HD)] = part[:, n * HD : (n + 1) * HD]
                head += 1

    wt = jnp.concatenate([wa[...], wb[...], wc[...], wd[...]], axis=1)
    projected = lax.dot_general(
        mine[...], wt, (((1,), (1,)), ((), ())), preferred_element_type=jnp.float32
    )
    projected = (projected + bias[...]).astype(jnp.bfloat16).astype(jnp.float32)
    out[...] = (residual[...].astype(jnp.float32) + gate[...] * projected).astype(jnp.bfloat16)


def project(parts, order, weights, bias, gate, residual):
    step = 512
    panel = pl.BlockSpec((step, QUARTER), lambda i: (i, 0))
    return pl.pallas_call(
        project_kernel,
        grid=(D // step,),
        out_shape=jax.ShapeDtypeStruct((ROWS, D), jnp.bfloat16),
        in_specs=[pl.BlockSpec(part.shape, lambda i: (0, 0)) for part in parts]
        + [pl.BlockSpec(memory_space=pltpu.SMEM)]
        + [panel] * 4
        + [
            pl.BlockSpec((1, step), lambda i: (0, i)),
            pl.BlockSpec((1, step), lambda i: (0, i)),
            pl.BlockSpec((ROWS, step), lambda i: (0, i)),
        ],
        out_specs=pl.BlockSpec((ROWS, step), lambda i: (0, i)),
        scratch_shapes=[
            pltpu.VMEM((ROWS, HID), jnp.bfloat16),
        ],
        compiler_params=pltpu.CompilerParams(vmem_limit_bytes=14 * 1024 * 1024),
        cost_estimate=pl.CostEstimate(
            flops=2 * ROWS * HID * D,
            bytes_accessed=2 * D * HID + 4 * ROWS * D,
            transcendentals=0,
        ),
        name="project",
    )(*parts, order, *weights, bias, gate, residual)


def stage(ready, work, *operands):
    shapes = jax.eval_shape(work, *operands)
    return lax.cond(
        ready,
        work,
        lambda *_: tuple(jnp.zeros(s.shape, s.dtype) for s in shapes),
        *operands,
    )


def local(
    queries,
    key_rows,
    value_rows,
    text_keys,
    text_values,
    residual,
    out_gate,
    out_weight,
    out_bias,
    tile_lists,
):
    seq, fsdp = lax.axis_index("seq"), lax.axis_index("fsdp")
    x, zh, c = seq // 4, seq // 2 % 2, seq % 2
    y, zl = fsdp // 4, fsdp % 4
    q = queries.reshape(ROWS, HID)
    k0, v0 = key_rows.reshape(ROWS, HID), value_rows.reshape(ROWS, HID)

    far_spot = jnp.where(zh == 0, seq - 2, seq + 2)
    spots = jnp.stack(
        [seq, seq ^ 1, seq ^ 2, seq ^ 3, far_spot, far_spot ^ 1]
    )
    inside = (spots >= 0) & (spots < 16)
    candidates = spots[:, None] + 16 * jnp.arange(GT, dtype=jnp.int32)[None, :]
    listed = tile_lists[0, :, 0, :]
    present = jnp.any(listed[:, None, None, :] == candidates[None, :, :, None], axis=3)
    present = present & inside[None, :, None]
    bias = jnp.where(present, 0.0, NEG).astype(jnp.float32).reshape(GT, 6 * GT)

    steps = jnp.array([0, 1, -1, 2], jnp.int32)
    firsts = [sum(GROUPS[:g]) for g in range(len(GROUPS))]
    packs = [pair(k0, v0, first, count) for first, count in zip(firsts, GROUPS)]

    def attend_group(g, near, others, far, text, far_other=None):
        return attend(
            bias,
            q,
            k0,
            v0,
            beside,
            (near, others),
            (far, others if far_other is None else far_other),
            text,
            firsts[g],
            GROUPS[g],
            far_other is None,
        )

    text = pair(text_keys[0], text_values[0], 0, 1, HID)
    piece = lax.dynamic_slice(
        out_weight.T, (0, (x % 2 * 2 + c) * QUARTER), (PANEL, QUARTER)
    )
    text_z = swap(text, 2)
    pack0, keys, values, wz1, wz2, wz3, text_z = lax.optimization_barrier(
        (
            packs[0],
            k0,
            v0,
            shift(piece, dz=1),
            shift(piece, dz=-1),
            shift(piece, dz=2),
            text_z,
        )
    )
    packs, bias, beside, wz1, wz2, wz3 = lax.optimization_barrier(
        (
            packs[1:],
            bias,
            shift(pair(keys, values, 0, HEADS), dc=1),
            wz1,
            wz2,
            wz3,
        )
    )
    near0 = shift(pack0, dz=4)
    packs = (pack0,) + tuple(packs)
    ready = tile_lists[0, 0, 0, 0] > -2

    def weight_stage(piece, wz1, wz2, wz3, text, text_z):
        wz = place_all((zl - steps) % 4, piece, wz1, wz2, wz3)
        wy1, text = lax.optimization_barrier((shift(wz, dy=1), join(text, text_z)))
        wy = place_all((y - steps) % 4, wz, wy1, shift(wz, dy=-1), shift(wz, dy=2))
        text = join(text, swap(text, 4))
        text = join(text, swap(text, 8))
        return wy.reshape(D, QUARTER), text

    wy, text = stage(ready, weight_stage, piece, wz1, wz2, wz3, text, text_z)
    pack1, wy = lax.optimization_barrier((packs[1], wy))
    near1 = shift(pack1, dz=4)
    near0, wy = lax.optimization_barrier((near0, wy))
    wx = across(wy)

    def first_stage(near0, text):
        far0 = forward(near0)
        text = join(text, swap(text, 1))
        return far0, shift(near0, dc=1), shift(far0, dc=1), text

    far0, near0_other, far0_other, text = stage(ready, first_stage, near0, text)

    def second_stage(near1, near0, near0_other, far0, far0_other, text):
        part0 = attend_group(0, near0, near0_other, far0, text, far0_other)
        near1_other = shift(near1, dc=1)
        far1, part0 = lax.optimization_barrier((forward(near1), part0))
        return part0, far1, near1_other, shift(far1, dc=1)

    pack2, near1, far0_other = lax.optimization_barrier((packs[2], near1, far0_other))
    near2 = shift(pack2, dz=4)
    part0, far1, near1_other, far1_other = stage(
        ready, second_stage, near1, near0, near0_other, far0, far0_other, text
    )

    def third_stage(near2, near1, near1_other, far1, far1_other, text, wy, wx):
        part1 = attend_group(1, near1, near1_other, far1, text, far1_other)
        wb, wd = shift(wy, dc=1), shift(wx, dc=1)
        far2, part1 = lax.optimization_barrier((forward(near2), part1))
        return part1, far2, shift(merge(near2, far2), dc=1), wb, wd

    pack3, near2, part0, wx = lax.optimization_barrier((packs[3], near2, part0, wx))
    near3 = shift(pack3, dz=4)
    part1, far2, others2, wb, wd = stage(
        ready,
        third_stage,
        near2,
        near1,
        near1_other,
        far1,
        far1_other,
        text,
        wy,
        wx,
    )
    near3, others2 = lax.optimization_barrier((near3, others2))
    part2 = attend_group(2, near2, others2, far2, text)
    far3, far3_other, near3_other, part2 = lax.optimization_barrier(
        (forward(near3), forward(near3, flip=1), shift(near3, dc=1), part2)
    )
    part3 = attend_group(3, near3, near3_other, far3, text, far3_other)
    parts = [part0, part1, part2, part3]
    own = x % 2 * 2 + c
    order = jnp.stack([own, own ^ 1, own ^ 2, own ^ 3]).astype(jnp.int32)
    weights = [w.reshape(-1, QUARTER) for w in (wy, wb, wx, wd)]
    mixed = project(
        parts,
        order,
        weights,
        out_bias.reshape(1, D),
        out_gate.reshape(1, D),
        residual.reshape(ROWS, D),
    )
    return mixed.reshape(residual.shape)


def solution(mesh):
    placed = (
        P("fsdp", None, "seq", None),
        P("fsdp", None, "seq", None),
        P("fsdp", None, "seq", None),
        P("fsdp", "seq", None),
        P("fsdp", "seq", None),
        P("fsdp", None, "seq", None),
        P(),
        P(None, "fsdp"),
        P(),
        P("fsdp", None, "seq", None),
    )
    return jax.shard_map(
        local, mesh=mesh, in_specs=placed, out_specs=P("fsdp", None, "seq", None), check_vma=False
    )
```

```python
import functools

import jax
import jax.numpy as jnp
from jax import lax
from jax.experimental import pallas as pl
from jax.experimental.pallas import tpu as pltpu
from jax.sharding import PartitionSpec as P

HEADS = 12
HD = 128
TILE = 128
GT = 3
ROWS = GT * TILE
HID = HEADS * HD
QUARTER = HID // 4
PANEL = 192
D = 3072
TEXT = 256
GROUPS = (6, 3, 2, 1)
NEG = -1e30
SCALE = HD**-0.5 * 1.4426950408889634
AXES = ("seq", "fsdp")


def place(x, y, z, c):
    return (((x % 4) * 2 + z % 8 // 4) * 2 + c % 2) * 16 + (y % 4) * 4 + z % 4


def shift(value, dx=0, dy=0, dz=0, dc=0):
    pairs = [
        (place(x, y, z, c), place(x + dx, y + dy, z + dz, c + dc))
        for x in range(4)
        for y in range(4)
        for z in range(8)
        for c in range(2)
    ]
    return lax.ppermute(value, AXES, pairs)


def forward(value, flip=0):
    pairs = [(s, ((s + 4) % 16 if s % 4 < 2 else (s - 4) % 16) ^ flip) for s in range(16)]
    return lax.ppermute(value, "seq", pairs)


def swap(value, bit):
    return lax.ppermute(value, "seq", [(s, s ^ bit) for s in range(16)])


def across(value):
    pairs = [(s, (s - 4) % 16 if s % 4 < 2 else (s + 4) % 16) for s in range(16)]
    return lax.ppermute(value, "seq", pairs)


def join_kernel(*refs):
    first = 0
    for ref in refs[:-1]:
        refs[-1][:, first : first + ref.shape[1], :] = ref[...]
        first += ref.shape[1]


def join(*pieces):
    rows = sum(p.shape[1] for p in pieces)
    return pl.pallas_call(
        join_kernel,
        out_shape=jax.ShapeDtypeStruct((2, rows, HID), jnp.bfloat16),
        compiler_params=pltpu.CompilerParams(vmem_limit_bytes=16 * 1024 * 1024),
        cost_estimate=pl.CostEstimate(
            flops=0, bytes_accessed=8 * rows * HID, transcendentals=0
        ),
        name="join",
    )(*pieces)


def pair_kernel(k, v, out):
    out[0] = k[...]
    out[1] = v[...]


def pair(k, v, first, count, width=HD):
    rows = k.shape[0]
    return pl.pallas_call(
        pair_kernel,
        grid=(count,),
        out_shape=jax.ShapeDtypeStruct((2, rows, count * width), jnp.bfloat16),
        in_specs=[pl.BlockSpec((rows, width), lambda i: (0, first + i))] * 2,
        out_specs=pl.BlockSpec((2, rows, width), lambda i: (0, 0, i)),
        compiler_params=pltpu.CompilerParams(vmem_limit_bytes=16 * 1024 * 1024),
        cost_estimate=pl.CostEstimate(
            flops=0, bytes_accessed=8 * rows * count * width, transcendentals=0
        ),
        name="pair",
    )(k, v)


def place_kernel(where, *refs):
    for n, ref in enumerate(refs[:-1]):
        refs[-1][where[n]] = ref[...]


def place_all(where, *pieces):
    shape = (4,) + pieces[0].shape
    size = 4 * pieces[0].size
    return pl.pallas_call(
        place_kernel,
        out_shape=jax.ShapeDtypeStruct(shape, jnp.bfloat16),
        in_specs=[pl.BlockSpec(memory_space=pltpu.SMEM)]
        + [pl.BlockSpec(memory_space=pltpu.VMEM)] * 4,
        compiler_params=pltpu.CompilerParams(vmem_limit_bytes=16 * 1024 * 1024),
        cost_estimate=pl.CostEstimate(flops=0, bytes_accessed=4 * size, transcendentals=0),
        name="place",
    )(where, *pieces)


def attend_kernel(bias, q, k0, v0, a1, b0, b1, c0, c1, words, out):
    contract = (((1,), (1,)), ((), ()))
    sources = [(k0, v0)] + [(r.at[0], r.at[1]) for r in (a1, b0, b1, c0, c1)]
    for t in range(GT):
        low, high = max(0, t - 1), min(GT, t + 2)
        qt = q[t * TILE : (t + 1) * TILE, :]
        pieces = []
        peak = None
        for n, (k, _) in enumerate(sources):
            s = lax.dot_general(
                qt, k[low * TILE : high * TILE, :], contract, preferred_element_type=jnp.float32
            )
            for j in range(low, high):
                part = s[:, (j - low) * TILE : (j - low + 1) * TILE] * SCALE + bias[t, n * GT + j]
                pieces.append(part)
                peak = part if peak is None else jnp.maximum(peak, part)
        s = lax.dot_general(qt, words[0], contract, preferred_element_type=jnp.float32) * SCALE
        for j in range(TEXT // TILE):
            part = s[:, j * TILE : (j + 1) * TILE]
            pieces.append(part)
            peak = jnp.maximum(peak, part)
        top = jnp.max(peak, axis=1, keepdims=True)
        total = jnp.zeros((TILE, TILE), jnp.float32)
        acc = jnp.zeros((TILE, HD), jnp.float32)
        at = 0
        for n in range(len(sources) + 1):
            if n < len(sources):
                count = high - low
                values = sources[n][1][low * TILE : high * TILE, :]
            else:
                count = TEXT // TILE
                values = words[1]
            weights = []
            for j in range(count):
                e = jnp.exp2(pieces[at + j] - top)
                total = total + e
                weights.append(e.astype(jnp.bfloat16))
            at += count
            acc = acc + jnp.dot(
                jnp.concatenate(weights, axis=1), values, preferred_element_type=jnp.float32
            )
        row = jnp.sum(total, axis=1, keepdims=True)
        out[t * TILE : (t + 1) * TILE, :] = (acc / row).astype(jnp.bfloat16)


def attend(bias, q, k0, v0, beside, near, far, text, first, count):
    wide = pl.BlockSpec((ROWS, HD), lambda i: (0, first + i))
    words = pl.BlockSpec((2, TEXT, HD), lambda i: (0, 0, first + i))
    pack = pl.BlockSpec((2, ROWS, HD), lambda i: (0, 0, i))
    whole = pl.BlockSpec((2, ROWS, HD), lambda i: (0, 0, first + i))
    units = 48 * count
    return pl.pallas_call(
        attend_kernel,
        grid=(count,),
        out_shape=jax.ShapeDtypeStruct((ROWS, count * HD), jnp.bfloat16),
        in_specs=[pl.BlockSpec(memory_space=pltpu.SMEM)]
        + [wide] * 3
        + [whole]
        + [pack] * 4
        + [words],
        out_specs=pl.BlockSpec((ROWS, HD), lambda i: (0, i)),
        compiler_params=pltpu.CompilerParams(vmem_limit_bytes=14 * 1024 * 1024),
        cost_estimate=pl.CostEstimate(
            flops=units * TILE * TILE * HD * 16,
            bytes_accessed=count * 2 * HD * (ROWS * 14 + TEXT * 2),
            transcendentals=units * TILE * TILE,
        ),
        name="attend",
    )(bias, q, k0, v0, beside, *near, *far, text)


def project_kernel(*refs):
    parts = refs[: len(GROUPS)]
    order, wa, wb, wc, wd, bias, gate, residual, out, mine = refs[
        len(GROUPS) :
    ]
    step = pl.program_id(0)

    @pl.when(step == 0)
    def _():
        head = 0
        for part in parts:
            for n in range(part.shape[1] // HD):
                column = pl.multiple_of(order[head // 3] * QUARTER + head % 3 * HD, HD)
                mine[:, pl.ds(column, HD)] = part[:, n * HD : (n + 1) * HD]
                head += 1

    wt = jnp.concatenate([wa[...], wb[...], wc[...], wd[...]], axis=1)
    projected = lax.dot_general(
        mine[...], wt, (((1,), (1,)), ((), ())), preferred_element_type=jnp.float32
    )
    projected = (projected + bias[...]).astype(jnp.bfloat16).astype(jnp.float32)
    out[...] = (residual[...].astype(jnp.float32) + gate[...] * projected).astype(jnp.bfloat16)


def project(parts, order, weights, bias, gate, residual):
    step = 512
    panel = pl.BlockSpec((step, QUARTER), lambda i: (i, 0))
    return pl.pallas_call(
        project_kernel,
        grid=(D // step,),
        out_shape=jax.ShapeDtypeStruct((ROWS, D), jnp.bfloat16),
        in_specs=[pl.BlockSpec(part.shape, lambda i: (0, 0)) for part in parts]
        + [pl.BlockSpec(memory_space=pltpu.SMEM)]
        + [panel] * 4
        + [
            pl.BlockSpec((1, step), lambda i: (0, i)),
            pl.BlockSpec((1, step), lambda i: (0, i)),
            pl.BlockSpec((ROWS, step), lambda i: (0, i)),
        ],
        out_specs=pl.BlockSpec((ROWS, step), lambda i: (0, i)),
        scratch_shapes=[
            pltpu.VMEM((ROWS, HID), jnp.bfloat16),
        ],
        compiler_params=pltpu.CompilerParams(vmem_limit_bytes=14 * 1024 * 1024),
        cost_estimate=pl.CostEstimate(
            flops=2 * ROWS * HID * D,
            bytes_accessed=2 * D * HID + 4 * ROWS * D,
            transcendentals=0,
        ),
        name="project",
    )(*parts, order, *weights, bias, gate, residual)


def stage(ready, work, *operands):
    shapes = jax.eval_shape(work, *operands)
    return lax.cond(
        ready,
        work,
        lambda *_: tuple(jnp.zeros(s.shape, s.dtype) for s in shapes),
        *operands,
    )


def local(
    queries,
    key_rows,
    value_rows,
    text_keys,
    text_values,
    residual,
    out_gate,
    out_weight,
    out_bias,
    tile_lists,
):
    seq, fsdp = lax.axis_index("seq"), lax.axis_index("fsdp")
    x, zh, c = seq // 4, seq // 2 % 2, seq % 2
    y, zl = fsdp // 4, fsdp % 4
    q = queries.reshape(ROWS, HID)
    k0, v0 = key_rows.reshape(ROWS, HID), value_rows.reshape(ROWS, HID)

    far_spot = jnp.where(zh == 0, seq - 2, seq + 2)
    spots = jnp.stack(
        [seq, seq ^ 1, seq ^ 2, seq ^ 3, far_spot, far_spot ^ 1]
    )
    inside = (spots >= 0) & (spots < 16)
    candidates = spots[:, None] + 16 * jnp.arange(GT, dtype=jnp.int32)[None, :]
    listed = tile_lists[0, :, 0, :]
    present = jnp.any(listed[:, None, None, :] == candidates[None, :, :, None], axis=3)
    present = present & inside[None, :, None]
    bias = jnp.where(present, 0.0, NEG).astype(jnp.float32).reshape(GT, 6 * GT)

    steps = jnp.array([0, 1, -1, 2], jnp.int32)
    firsts = [sum(GROUPS[:g]) for g in range(len(GROUPS))]
    packs = [pair(k0, v0, first, count) for first, count in zip(firsts, GROUPS)]

    def attend_group(g, near, near_other, far, text, far_other):
        return attend(
            bias,
            q,
            k0,
            v0,
            beside,
            (near, near_other),
            (far, far_other),
            text,
            firsts[g],
            GROUPS[g],
        )

    text = pair(text_keys[0], text_values[0], 0, 1, HID)
    piece = lax.dynamic_slice(
        out_weight.T, (0, (x % 2 * 2 + c) * QUARTER), (PANEL, QUARTER)
    )
    text_z = swap(text, 2)
    pack0, keys, values, wz1, wz2, wz3, text_z = lax.optimization_barrier(
        (
            packs[0],
            k0,
            v0,
            shift(piece, dz=1),
            shift(piece, dz=-1),
            shift(piece, dz=2),
            text_z,
        )
    )
    packs, bias, beside, wz1, wz2, wz3 = lax.optimization_barrier(
        (
            packs[1:],
            bias,
            shift(pair(keys, values, 0, HEADS), dc=1),
            wz1,
            wz2,
            wz3,
        )
    )
    near0 = shift(pack0, dz=4)
    packs = (pack0,) + tuple(packs)
    ready = tile_lists[0, 0, 0, 0] > -2

    def weight_stage(piece, wz1, wz2, wz3, text, text_z):
        wz = place_all((zl - steps) % 4, piece, wz1, wz2, wz3)
        wy1, text = lax.optimization_barrier((shift(wz, dy=1), join(text, text_z)))
        wy = place_all((y - steps) % 4, wz, wy1, shift(wz, dy=-1), shift(wz, dy=2))
        text = join(text, swap(text, 4))
        text = join(text, swap(text, 8))
        return wy.reshape(D, QUARTER), text

    wy, text = stage(ready, weight_stage, piece, wz1, wz2, wz3, text, text_z)
    pack1, wy = lax.optimization_barrier((packs[1], wy))
    near1 = shift(pack1, dz=4)
    near0, wy = lax.optimization_barrier((near0, wy))
    wx = across(wy)

    def first_stage(near0, text):
        far0 = forward(near0)
        text = join(text, swap(text, 1))
        return far0, shift(near0, dc=1), shift(far0, dc=1), text

    far0, near0_other, far0_other, text = stage(ready, first_stage, near0, text)

    def second_stage(near1, near0, near0_other, far0, far0_other, text):
        part0 = attend_group(0, near0, near0_other, far0, text, far0_other)
        near1_other = shift(near1, dc=1)
        far1, part0 = lax.optimization_barrier((forward(near1), part0))
        return part0, far1, near1_other, shift(far1, dc=1)

    pack2, near1, far0_other = lax.optimization_barrier((packs[2], near1, far0_other))
    near2 = shift(pack2, dz=4)
    part0, far1, near1_other, far1_other = stage(
        ready, second_stage, near1, near0, near0_other, far0, far0_other, text
    )

    def third_stage(near2, near1, near1_other, far1, far1_other, text, wy):
        part1 = attend_group(1, near1, near1_other, far1, text, far1_other)
        near2_other, wb = shift(near2, dc=1), shift(wy, dc=1)
        far2, part1 = lax.optimization_barrier((forward(near2), part1))
        return part1, near2_other, far2, shift(far2, dc=1), wb

    pack3, near2, part0 = lax.optimization_barrier((packs[3], near2, part0))
    near3 = shift(pack3, dz=4)
    part1, near2_other, far2, far2_other, wb = stage(
        ready,
        third_stage,
        near2,
        near1,
        near1_other,
        far1,
        far1_other,
        text,
        wy,
    )
    near3, near2_other, wx = lax.optimization_barrier((near3, near2_other, wx))
    wd = shift(wx, dc=1)
    part2 = attend_group(2, near2, near2_other, far2, text, far2_other)
    far3, far3_other, near3_other, part2 = lax.optimization_barrier(
        (forward(near3), forward(near3, flip=1), shift(near3, dc=1), part2)
    )
    part3 = attend_group(3, near3, near3_other, far3, text, far3_other)
    parts = [part0, part1, part2, part3]
    own = x % 2 * 2 + c
    order = jnp.stack([own, own ^ 1, own ^ 2, own ^ 3]).astype(jnp.int32)
    weights = [w.reshape(-1, QUARTER) for w in (wy, wb, wx, wd)]
    mixed = project(
        parts,
        order,
        weights,
        out_bias.reshape(1, D),
        out_gate.reshape(1, D),
        residual.reshape(ROWS, D),
    )
    return mixed.reshape(residual.shape)


def solution(mesh):
    placed = (
        P("fsdp", None, "seq", None),
        P("fsdp", None, "seq", None),
        P("fsdp", None, "seq", None),
        P("fsdp", "seq", None),
        P("fsdp", "seq", None),
        P("fsdp", None, "seq", None),
        P(),
        P(None, "fsdp"),
        P(),
        P("fsdp", None, "seq", None),
    )
    return jax.shard_map(
        local, mesh=mesh, in_specs=placed, out_specs=P("fsdp", None, "seq", None), check_vma=False
    )
```

```python
import functools

import jax
import jax.numpy as jnp
from jax import lax
from jax.experimental import pallas as pl
from jax.experimental.pallas import tpu as pltpu
from jax.sharding import PartitionSpec as P

HEADS = 12
HD = 128
TILE = 128
GT = 3
ROWS = GT * TILE
HID = HEADS * HD
QUARTER = HID // 4
PANEL = 192
D = 3072
TEXT = 256
GROUPS = (6, 3, 2, 1)
NEG = -1e30
SCALE = HD**-0.5 * 1.4426950408889634
AXES = ("seq", "fsdp")


def place(x, y, z, c):
    return (((x % 4) * 2 + z % 8 // 4) * 2 + c % 2) * 16 + (y % 4) * 4 + z % 4


def shift(value, dx=0, dy=0, dz=0, dc=0):
    pairs = [
        (place(x, y, z, c), place(x + dx, y + dy, z + dz, c + dc))
        for x in range(4)
        for y in range(4)
        for z in range(8)
        for c in range(2)
    ]
    return lax.ppermute(value, AXES, pairs)


def forward(value, flip=0):
    pairs = [(s, ((s + 4) % 16 if s % 4 < 2 else (s - 4) % 16) ^ flip) for s in range(16)]
    return lax.ppermute(value, "seq", pairs)


def swap(value, bit):
    return lax.ppermute(value, "seq", [(s, s ^ bit) for s in range(16)])


def across(value):
    pairs = [(s, (s - 4) % 16 if s % 4 < 2 else (s + 4) % 16) for s in range(16)]
    return lax.ppermute(value, "seq", pairs)


def join_kernel(*refs):
    first = 0
    for ref in refs[:-1]:
        refs[-1][:, first : first + ref.shape[1], :] = ref[...]
        first += ref.shape[1]


def join(*pieces):
    rows = sum(p.shape[1] for p in pieces)
    return pl.pallas_call(
        join_kernel,
        out_shape=jax.ShapeDtypeStruct((2, rows, HID), jnp.bfloat16),
        compiler_params=pltpu.CompilerParams(vmem_limit_bytes=16 * 1024 * 1024),
        cost_estimate=pl.CostEstimate(
            flops=0, bytes_accessed=8 * rows * HID, transcendentals=0
        ),
        name="join",
    )(*pieces)


def pair_kernel(k, v, out):
    out[0] = k[...]
    out[1] = v[...]


def pair(k, v, first, count, width=HD):
    rows = k.shape[0]
    return pl.pallas_call(
        pair_kernel,
        grid=(count,),
        out_shape=jax.ShapeDtypeStruct((2, rows, count * width), jnp.bfloat16),
        in_specs=[pl.BlockSpec((rows, width), lambda i: (0, first + i))] * 2,
        out_specs=pl.BlockSpec((2, rows, width), lambda i: (0, 0, i)),
        compiler_params=pltpu.CompilerParams(vmem_limit_bytes=16 * 1024 * 1024),
        cost_estimate=pl.CostEstimate(
            flops=0, bytes_accessed=8 * rows * count * width, transcendentals=0
        ),
        name="pair",
    )(k, v)


def place_kernel(where, *refs):
    for n, ref in enumerate(refs[:-1]):
        refs[-1][where[n]] = ref[...]


def place_all(where, *pieces):
    shape = (4,) + pieces[0].shape
    size = 4 * pieces[0].size
    return pl.pallas_call(
        place_kernel,
        out_shape=jax.ShapeDtypeStruct(shape, jnp.bfloat16),
        in_specs=[pl.BlockSpec(memory_space=pltpu.SMEM)]
        + [pl.BlockSpec(memory_space=pltpu.VMEM)] * 4,
        compiler_params=pltpu.CompilerParams(vmem_limit_bytes=16 * 1024 * 1024),
        cost_estimate=pl.CostEstimate(flops=0, bytes_accessed=4 * size, transcendentals=0),
        name="place",
    )(where, *pieces)


def attend_kernel(bias, q, k0, v0, a1, b0, b1, c0, c1, t0, t1, out):
    contract = (((1,), (1,)), ((), ()))
    sources = [(k0, v0)] + [(r.at[0], r.at[1]) for r in (a1, b0, b1, c0, c1)]
    for t in range(GT):
        low, high = max(0, t - 1), min(GT, t + 2)
        qt = q[t * TILE : (t + 1) * TILE, :]
        pieces = []
        peak = None
        for n, (k, _) in enumerate(sources):
            s = lax.dot_general(
                qt, k[low * TILE : high * TILE, :], contract, preferred_element_type=jnp.float32
            )
            for j in range(low, high):
                part = s[:, (j - low) * TILE : (j - low + 1) * TILE] * SCALE + bias[t, n * GT + j]
                pieces.append(part)
                peak = part if peak is None else jnp.maximum(peak, part)
        words = jnp.concatenate([t0[0], t1[0]], axis=0)
        s = lax.dot_general(qt, words, contract, preferred_element_type=jnp.float32) * SCALE
        for j in range(TEXT // TILE):
            part = s[:, j * TILE : (j + 1) * TILE]
            pieces.append(part)
            peak = jnp.maximum(peak, part)
        top = jnp.max(peak, axis=1, keepdims=True)
        total = jnp.zeros((TILE, TILE), jnp.float32)
        acc = jnp.zeros((TILE, HD), jnp.float32)
        at = 0
        for n in range(len(sources) + 1):
            if n < len(sources):
                count = high - low
                values = sources[n][1][low * TILE : high * TILE, :]
            else:
                count = TEXT // TILE
                values = jnp.concatenate([t0[1], t1[1]], axis=0)
            weights = []
            for j in range(count):
                e = jnp.exp2(pieces[at + j] - top)
                total = total + e
                weights.append(e.astype(jnp.bfloat16))
            at += count
            acc = acc + jnp.dot(
                jnp.concatenate(weights, axis=1), values, preferred_element_type=jnp.float32
            )
        row = jnp.sum(total, axis=1, keepdims=True)
        out[t * TILE : (t + 1) * TILE, :] = (acc / row).astype(jnp.bfloat16)


def attend(bias, q, k0, v0, beside, near, far, text, first, count):
    wide = pl.BlockSpec((ROWS, HD), lambda i: (0, first + i))
    words = pl.BlockSpec((2, TEXT // 2, HD), lambda i: (0, 0, first + i))
    pack = pl.BlockSpec((2, ROWS, HD), lambda i: (0, 0, i))
    whole = pl.BlockSpec((2, ROWS, HD), lambda i: (0, 0, first + i))
    units = 48 * count
    return pl.pallas_call(
        attend_kernel,
        grid=(count,),
        out_shape=jax.ShapeDtypeStruct((ROWS, count * HD), jnp.bfloat16),
        in_specs=[pl.BlockSpec(memory_space=pltpu.SMEM)]
        + [wide] * 3
        + [whole]
        + [pack] * 4
        + [words] * 2,
        out_specs=pl.BlockSpec((ROWS, HD), lambda i: (0, i)),
        compiler_params=pltpu.CompilerParams(vmem_limit_bytes=14 * 1024 * 1024),
        cost_estimate=pl.CostEstimate(
            flops=units * TILE * TILE * HD * 16,
            bytes_accessed=count * 2 * HD * (ROWS * 14 + TEXT * 2),
            transcendentals=units * TILE * TILE,
        ),
        name="attend",
    )(bias, q, k0, v0, beside, *near, *far, *text)


def project_kernel(*refs):
    parts = refs[: len(GROUPS)]
    order, wa, wb, wc, wd, bias, gate, residual, out, mine = refs[
        len(GROUPS) :
    ]
    step = pl.program_id(0)

    @pl.when(step == 0)
    def _():
        head = 0
        for part in parts:
            for n in range(part.shape[1] // HD):
                column = pl.multiple_of(order[head // 3] * QUARTER + head % 3 * HD, HD)
                mine[:, pl.ds(column, HD)] = part[:, n * HD : (n + 1) * HD]
                head += 1

    wt = jnp.concatenate([wa[...], wb[...], wc[...], wd[...]], axis=1)
    projected = lax.dot_general(
        mine[...], wt, (((1,), (1,)), ((), ())), preferred_element_type=jnp.float32
    )
    projected = (projected + bias[...]).astype(jnp.bfloat16).astype(jnp.float32)
    out[...] = (residual[...].astype(jnp.float32) + gate[...] * projected).astype(jnp.bfloat16)


def project(parts, order, weights, bias, gate, residual):
    step = 768
    panel = pl.BlockSpec((step, QUARTER), lambda i: (i, 0))
    return pl.pallas_call(
        project_kernel,
        grid=(D // step,),
        out_shape=jax.ShapeDtypeStruct((ROWS, D), jnp.bfloat16),
        in_specs=[pl.BlockSpec(part.shape, lambda i: (0, 0)) for part in parts]
        + [pl.BlockSpec(memory_space=pltpu.SMEM)]
        + [panel] * 4
        + [
            pl.BlockSpec((1, step), lambda i: (0, i)),
            pl.BlockSpec((1, step), lambda i: (0, i)),
            pl.BlockSpec((ROWS, step), lambda i: (0, i)),
        ],
        out_specs=pl.BlockSpec((ROWS, step), lambda i: (0, i)),
        scratch_shapes=[
            pltpu.VMEM((ROWS, HID), jnp.bfloat16),
        ],
        compiler_params=pltpu.CompilerParams(vmem_limit_bytes=24 * 1024 * 1024),
        cost_estimate=pl.CostEstimate(
            flops=2 * ROWS * HID * D,
            bytes_accessed=2 * D * HID + 4 * ROWS * D,
            transcendentals=0,
        ),
        name="project",
    )(*parts, order, *weights, bias, gate, residual)


def stage(ready, work, *operands):
    shapes = jax.eval_shape(work, *operands)
    return lax.cond(
        ready,
        work,
        lambda *_: tuple(jnp.zeros(s.shape, s.dtype) for s in shapes),
        *operands,
    )


def local(
    queries,
    key_rows,
    value_rows,
    text_keys,
    text_values,
    residual,
    out_gate,
    out_weight,
    out_bias,
    tile_lists,
):
    seq, fsdp = lax.axis_index("seq"), lax.axis_index("fsdp")
    x, zh, c = seq // 4, seq // 2 % 2, seq % 2
    y, zl = fsdp // 4, fsdp % 4
    q = queries.reshape(ROWS, HID)
    k0, v0 = key_rows.reshape(ROWS, HID), value_rows.reshape(ROWS, HID)

    far_spot = jnp.where(zh == 0, seq - 2, seq + 2)
    spots = jnp.stack(
        [seq, seq ^ 1, seq ^ 2, seq ^ 3, far_spot, far_spot ^ 1]
    )
    inside = (spots >= 0) & (spots < 16)
    candidates = spots[:, None] + 16 * jnp.arange(GT, dtype=jnp.int32)[None, :]
    listed = tile_lists[0, :, 0, :]
    present = jnp.any(listed[:, None, None, :] == candidates[None, :, :, None], axis=3)
    present = present & inside[None, :, None]
    bias = jnp.where(present, 0.0, NEG).astype(jnp.float32).reshape(GT, 6 * GT)

    steps = jnp.array([0, 1, -1, 2], jnp.int32)
    firsts = [sum(GROUPS[:g]) for g in range(len(GROUPS))]
    packs = [pair(k0, v0, first, count) for first, count in zip(firsts, GROUPS)]

    def attend_group(g, near, near_other, far, text, far_other):
        return attend(
            bias,
            q,
            k0,
            v0,
            beside,
            (near, near_other),
            (far, far_other),
            text,
            firsts[g],
            GROUPS[g],
        )

    text = pair(text_keys[0], text_values[0], 0, 1, HID)
    piece = lax.dynamic_slice(
        out_weight.T, (0, (x % 2 * 2 + c) * QUARTER), (PANEL, QUARTER)
    )
    text_z = swap(text, 2)
    pack0, keys, values, wz1, wz2, wz3, text_z = lax.optimization_barrier(
        (
            packs[0],
            k0,
            v0,
            shift(piece, dz=1),
            shift(piece, dz=-1),
            shift(piece, dz=2),
            text_z,
        )
    )
    packs, bias, beside, wz1, wz2, wz3 = lax.optimization_barrier(
        (
            packs[1:],
            bias,
            shift(pair(keys, values, 0, HEADS), dc=1),
            wz1,
            wz2,
            wz3,
        )
    )
    near0 = shift(pack0, dz=4)
    packs = (pack0,) + tuple(packs)
    ready = tile_lists[0, 0, 0, 0] > -2

    def weight_stage(piece, wz1, wz2, wz3, text, text_z):
        wz = place_all((zl - steps) % 4, piece, wz1, wz2, wz3)
        wy1, text = lax.optimization_barrier((shift(wz, dy=1), join(text, text_z)))
        wy = place_all((y - steps) % 4, wz, wy1, shift(wz, dy=-1), shift(wz, dy=2))
        text = join(text, swap(text, 4))
        text = join(text, swap(text, 8))
        return wy.reshape(D, QUARTER), text

    wy, text = stage(ready, weight_stage, piece, wz1, wz2, wz3, text, text_z)
    pack1, wy = lax.optimization_barrier((packs[1], wy))
    near1 = shift(pack1, dz=4)
    near0, wy = lax.optimization_barrier((near0, wy))
    wx = across(wy)

    def first_stage(near0, text):
        near0_other = shift(near0, dc=1)
        far0, text = lax.optimization_barrier((forward(near0), swap(text, 1)))
        return far0, near0_other, shift(far0, dc=1), text

    far0, near0_other, far0_other, text_other = stage(ready, first_stage, near0, text)
    text = (text, text_other)

    def second_stage(near1, near0, near0_other, far0, far0_other, text):
        part0 = attend_group(0, near0, near0_other, far0, text, far0_other)
        near1_other = shift(near1, dc=1)
        far1, part0 = lax.optimization_barrier((forward(near1), part0))
        return part0, far1, near1_other, shift(far1, dc=1)

    pack2, near1, far0_other = lax.optimization_barrier((packs[2], near1, far0_other))
    near2 = shift(pack2, dz=4)
    part0, far1, near1_other, far1_other = stage(
        ready, second_stage, near1, near0, near0_other, far0, far0_other, text
    )

    def third_stage(near2, near1, near1_other, far1, far1_other, text, wy, wx):
        part1 = attend_group(1, near1, near1_other, far1, text, far1_other)
        near2_other, wb, wd = shift(near2, dc=1), shift(wy, dc=1), shift(wx, dc=1)
        far2, part1 = lax.optimization_barrier((forward(near2), part1))
        return part1, near2_other, far2, shift(far2, dc=1), wb, wd

    pack3, near2, part0, wx = lax.optimization_barrier((packs[3], near2, part0, wx))
    near3 = shift(pack3, dz=4)
    part1, near2_other, far2, far2_other, wb, wd = stage(
        ready,
        third_stage,
        near2,
        near1,
        near1_other,
        far1,
        far1_other,
        text,
        wy,
        wx,
    )
    near3, near2_other = lax.optimization_barrier((near3, near2_other))
    part2 = attend_group(2, near2, near2_other, far2, text, far2_other)
    far3, far3_other, near3_other, part2 = lax.optimization_barrier(
        (forward(near3), forward(near3, flip=1), shift(near3, dc=1), part2)
    )
    part3 = attend_group(3, near3, near3_other, far3, text, far3_other)
    parts = [part0, part1, part2, part3]
    own = x % 2 * 2 + c
    order = jnp.stack([own, own ^ 1, own ^ 2, own ^ 3]).astype(jnp.int32)
    weights = [w.reshape(-1, QUARTER) for w in (wy, wb, wx, wd)]
    mixed = project(
        parts,
        order,
        weights,
        out_bias.reshape(1, D),
        out_gate.reshape(1, D),
        residual.reshape(ROWS, D),
    )
    return mixed.reshape(residual.shape)


def solution(mesh):
    placed = (
        P("fsdp", None, "seq", None),
        P("fsdp", None, "seq", None),
        P("fsdp", None, "seq", None),
        P("fsdp", "seq", None),
        P("fsdp", "seq", None),
        P("fsdp", None, "seq", None),
        P(),
        P(None, "fsdp"),
        P(),
        P("fsdp", None, "seq", None),
    )
    return jax.shard_map(
        local, mesh=mesh, in_specs=placed, out_specs=P("fsdp", None, "seq", None), check_vma=False
    )
```

```python
import functools

import jax
import jax.numpy as jnp
from jax import lax
from jax.experimental import pallas as pl
from jax.experimental.pallas import tpu as pltpu
from jax.sharding import PartitionSpec as P

HEADS = 12
HD = 128
TILE = 128
GT = 3
ROWS = GT * TILE
HID = HEADS * HD
QUARTER = HID // 4
PANEL = 192
D = 3072
TEXT = 256
GROUPS = (5, 3, 3, 1)
NEG = -1e30
SCALE = HD**-0.5 * 1.4426950408889634
AXES = ("seq", "fsdp")


def place(x, y, z, c):
    return (((x % 4) * 2 + z % 8 // 4) * 2 + c % 2) * 16 + (y % 4) * 4 + z % 4


def shift(value, dx=0, dy=0, dz=0, dc=0):
    pairs = [
        (place(x, y, z, c), place(x + dx, y + dy, z + dz, c + dc))
        for x in range(4)
        for y in range(4)
        for z in range(8)
        for c in range(2)
    ]
    return lax.ppermute(value, AXES, pairs)


def forward(value, flip=0):
    pairs = [(s, ((s + 4) % 16 if s % 4 < 2 else (s - 4) % 16) ^ flip) for s in range(16)]
    return lax.ppermute(value, "seq", pairs)


def swap(value, bit):
    return lax.ppermute(value, "seq", [(s, s ^ bit) for s in range(16)])


def across(value):
    pairs = [(s, (s - 4) % 16 if s % 4 < 2 else (s + 4) % 16) for s in range(16)]
    return lax.ppermute(value, "seq", pairs)


def join_kernel(*refs):
    first = 0
    for ref in refs[:-1]:
        refs[-1][:, first : first + ref.shape[1], :] = ref[...]
        first += ref.shape[1]


def join(*pieces):
    rows = sum(p.shape[1] for p in pieces)
    return pl.pallas_call(
        join_kernel,
        out_shape=jax.ShapeDtypeStruct((2, rows, HID), jnp.bfloat16),
        compiler_params=pltpu.CompilerParams(vmem_limit_bytes=16 * 1024 * 1024),
        cost_estimate=pl.CostEstimate(
            flops=0, bytes_accessed=8 * rows * HID, transcendentals=0
        ),
        name="join",
    )(*pieces)


def pair_kernel(k, v, out):
    out[0] = k[...]
    out[1] = v[...]


def pair(k, v, first, count, width=HD):
    rows = k.shape[0]
    return pl.pallas_call(
        pair_kernel,
        grid=(count,),
        out_shape=jax.ShapeDtypeStruct((2, rows, count * width), jnp.bfloat16),
        in_specs=[pl.BlockSpec((rows, width), lambda i: (0, first + i))] * 2,
        out_specs=pl.BlockSpec((2, rows, width), lambda i: (0, 0, i)),
        compiler_params=pltpu.CompilerParams(vmem_limit_bytes=16 * 1024 * 1024),
        cost_estimate=pl.CostEstimate(
            flops=0, bytes_accessed=8 * rows * count * width, transcendentals=0
        ),
        name="pair",
    )(k, v)


def place_kernel(where, *refs):
    for n, ref in enumerate(refs[:-1]):
        refs[-1][where[n]] = ref[...]


def place_all(where, *pieces):
    shape = (4,) + pieces[0].shape
    size = 4 * pieces[0].size
    return pl.pallas_call(
        place_kernel,
        out_shape=jax.ShapeDtypeStruct(shape, jnp.bfloat16),
        in_specs=[pl.BlockSpec(memory_space=pltpu.SMEM)]
        + [pl.BlockSpec(memory_space=pltpu.VMEM)] * 4,
        compiler_params=pltpu.CompilerParams(vmem_limit_bytes=16 * 1024 * 1024),
        cost_estimate=pl.CostEstimate(flops=0, bytes_accessed=4 * size, transcendentals=0),
        name="place",
    )(where, *pieces)


def attend_kernel(bias, q, k0, v0, a1, b0, b1, c0, c1, t0, t1, out):
    contract = (((1,), (1,)), ((), ()))
    sources = [(k0, v0)] + [(r.at[0], r.at[1]) for r in (a1, b0, b1, c0, c1)]
    for t in range(GT):
        low, high = max(0, t - 1), min(GT, t + 2)
        qt = q[t * TILE : (t + 1) * TILE, :]
        pieces = []
        peak = None
        for n, (k, _) in enumerate(sources):
            s = lax.dot_general(
                qt, k[low * TILE : high * TILE, :], contract, preferred_element_type=jnp.float32
            )
            for j in range(low, high):
                part = s[:, (j - low) * TILE : (j - low + 1) * TILE] * SCALE + bias[t, n * GT + j]
                pieces.append(part)
                peak = part if peak is None else jnp.maximum(peak, part)
        words = jnp.concatenate([t0[0], t1[0]], axis=0)
        s = lax.dot_general(qt, words, contract, preferred_element_type=jnp.float32) * SCALE
        for j in range(TEXT // TILE):
            part = s[:, j * TILE : (j + 1) * TILE]
            pieces.append(part)
            peak = jnp.maximum(peak, part)
        top = jnp.max(peak, axis=1, keepdims=True)
        total = jnp.zeros((TILE, TILE), jnp.float32)
        acc = jnp.zeros((TILE, HD), jnp.float32)
        at = 0
        for n in range(len(sources) + 1):
            if n < len(sources):
                count = high - low
                values = sources[n][1][low * TILE : high * TILE, :]
            else:
                count = TEXT // TILE
                values = jnp.concatenate([t0[1], t1[1]], axis=0)
            weights = []
            for j in range(count):
                e = jnp.exp2(pieces[at + j] - top)
                total = total + e
                weights.append(e.astype(jnp.bfloat16))
            at += count
            acc = acc + jnp.dot(
                jnp.concatenate(weights, axis=1), values, preferred_element_type=jnp.float32
            )
        row = jnp.sum(total, axis=1, keepdims=True)
        out[t * TILE : (t + 1) * TILE, :] = (acc / row).astype(jnp.bfloat16)


def attend(bias, q, k0, v0, beside, near, far, text, first, count):
    wide = pl.BlockSpec((ROWS, HD), lambda i: (0, first + i))
    words = pl.BlockSpec((2, TEXT // 2, HD), lambda i: (0, 0, first + i))
    pack = pl.BlockSpec((2, ROWS, HD), lambda i: (0, 0, i))
    whole = pl.BlockSpec((2, ROWS, HD), lambda i: (0, 0, first + i))
    units = 48 * count
    return pl.pallas_call(
        attend_kernel,
        grid=(count,),
        out_shape=jax.ShapeDtypeStruct((ROWS, count * HD), jnp.bfloat16),
        in_specs=[pl.BlockSpec(memory_space=pltpu.SMEM)]
        + [wide] * 3
        + [whole]
        + [pack] * 4
        + [words] * 2,
        out_specs=pl.BlockSpec((ROWS, HD), lambda i: (0, i)),
        compiler_params=pltpu.CompilerParams(vmem_limit_bytes=14 * 1024 * 1024),
        cost_estimate=pl.CostEstimate(
            flops=units * TILE * TILE * HD * 16,
            bytes_accessed=count * 2 * HD * (ROWS * 14 + TEXT * 2),
            transcendentals=units * TILE * TILE,
        ),
        name="attend",
    )(bias, q, k0, v0, beside, *near, *far, *text)


def project_kernel(*refs):
    parts = refs[: len(GROUPS)]
    order, wa, wb, wc, wd, bias, gate, residual, out, mine = refs[
        len(GROUPS) :
    ]
    step = pl.program_id(0)

    @pl.when(step == 0)
    def _():
        head = 0
        for part in parts:
            for n in range(part.shape[1] // HD):
                column = pl.multiple_of(order[head // 3] * QUARTER + head % 3 * HD, HD)
                mine[:, pl.ds(column, HD)] = part[:, n * HD : (n + 1) * HD]
                head += 1

    wt = jnp.concatenate([wa[...], wb[...], wc[...], wd[...]], axis=1)
    projected = lax.dot_general(
        mine[...], wt, (((1,), (1,)), ((), ())), preferred_element_type=jnp.float32
    )
    projected = (projected + bias[...]).astype(jnp.bfloat16).astype(jnp.float32)
    out[...] = (residual[...].astype(jnp.float32) + gate[...] * projected).astype(jnp.bfloat16)


def project(parts, order, weights, bias, gate, residual):
    step = 768
    panel = pl.BlockSpec((step, QUARTER), lambda i: (i, 0))
    return pl.pallas_call(
        project_kernel,
        grid=(D // step,),
        out_shape=jax.ShapeDtypeStruct((ROWS, D), jnp.bfloat16),
        in_specs=[pl.BlockSpec(part.shape, lambda i: (0, 0)) for part in parts]
        + [pl.BlockSpec(memory_space=pltpu.SMEM)]
        + [panel] * 4
        + [
            pl.BlockSpec((1, step), lambda i: (0, i)),
            pl.BlockSpec((1, step), lambda i: (0, i)),
            pl.BlockSpec((ROWS, step), lambda i: (0, i)),
        ],
        out_specs=pl.BlockSpec((ROWS, step), lambda i: (0, i)),
        scratch_shapes=[
            pltpu.VMEM((ROWS, HID), jnp.bfloat16),
        ],
        compiler_params=pltpu.CompilerParams(vmem_limit_bytes=24 * 1024 * 1024),
        cost_estimate=pl.CostEstimate(
            flops=2 * ROWS * HID * D,
            bytes_accessed=2 * D * HID + 4 * ROWS * D,
            transcendentals=0,
        ),
        name="project",
    )(*parts, order, *weights, bias, gate, residual)


def stage(ready, work, *operands):
    shapes = jax.eval_shape(work, *operands)
    return lax.cond(
        ready,
        work,
        lambda *_: tuple(jnp.zeros(s.shape, s.dtype) for s in shapes),
        *operands,
    )


def local(
    queries,
    key_rows,
    value_rows,
    text_keys,
    text_values,
    residual,
    out_gate,
    out_weight,
    out_bias,
    tile_lists,
):
    seq, fsdp = lax.axis_index("seq"), lax.axis_index("fsdp")
    x, zh, c = seq // 4, seq // 2 % 2, seq % 2
    y, zl = fsdp // 4, fsdp % 4
    q = queries.reshape(ROWS, HID)
    k0, v0 = key_rows.reshape(ROWS, HID), value_rows.reshape(ROWS, HID)

    far_spot = jnp.where(zh == 0, seq - 2, seq + 2)
    spots = jnp.stack(
        [seq, seq ^ 1, seq ^ 2, seq ^ 3, far_spot, far_spot ^ 1]
    )
    inside = (spots >= 0) & (spots < 16)
    candidates = spots[:, None] + 16 * jnp.arange(GT, dtype=jnp.int32)[None, :]
    listed = tile_lists[0, :, 0, :]
    present = jnp.any(listed[:, None, None, :] == candidates[None, :, :, None], axis=3)
    present = present & inside[None, :, None]
    bias = jnp.where(present, 0.0, NEG).astype(jnp.float32).reshape(GT, 6 * GT)

    steps = jnp.array([0, 1, -1, 2], jnp.int32)
    firsts = [sum(GROUPS[:g]) for g in range(len(GROUPS))]
    packs = [pair(k0, v0, first, count) for first, count in zip(firsts, GROUPS)]

    def attend_group(g, near, near_other, far, text, far_other):
        return attend(
            bias,
            q,
            k0,
            v0,
            beside,
            (near, near_other),
            (far, far_other),
            text,
            firsts[g],
            GROUPS[g],
        )

    text = pair(text_keys[0], text_values[0], 0, 1, HID)
    piece = lax.dynamic_slice(
        out_weight.T, (0, (x % 2 * 2 + c) * QUARTER), (PANEL, QUARTER)
    )
    text_z = swap(text, 2)
    pack0, keys, values, wz1, wz2, wz3, text_z = lax.optimization_barrier(
        (
            packs[0],
            k0,
            v0,
            shift(piece, dz=1),
            shift(piece, dz=-1),
            shift(piece, dz=2),
            text_z,
        )
    )
    packs, bias, beside, wz1, wz2, wz3 = lax.optimization_barrier(
        (
            packs[1:],
            bias,
            shift(pair(keys, values, 0, HEADS), dc=1),
            wz1,
            wz2,
            wz3,
        )
    )
    near0 = shift(pack0, dz=4)
    packs = (pack0,) + tuple(packs)
    ready = tile_lists[0, 0, 0, 0] > -2

    def weight_stage(piece, wz1, wz2, wz3, text, text_z):
        wz = place_all((zl - steps) % 4, piece, wz1, wz2, wz3)
        wy1, text = lax.optimization_barrier((shift(wz, dy=1), join(text, text_z)))
        wy = place_all((y - steps) % 4, wz, wy1, shift(wz, dy=-1), shift(wz, dy=2))
        text = join(text, swap(text, 4))
        text = join(text, swap(text, 8))
        return wy.reshape(D, QUARTER), text

    wy, text = stage(ready, weight_stage, piece, wz1, wz2, wz3, text, text_z)
    pack1, wy = lax.optimization_barrier((packs[1], wy))
    near1 = shift(pack1, dz=4)
    near0, wy, pack2 = lax.optimization_barrier((near0, wy, packs[2]))
    near2 = shift(pack2, dz=4)
    wx = across(wy)

    def first_stage(near0):
        far0 = forward(near0)
        return far0, shift(near0, dc=1), shift(far0, dc=1)

    far0, near0_other, far0_other = stage(ready, first_stage, near0)

    def second_stage(near1, near0, near0_other, far0, far0_other, text):
        text_other = swap(text, 1)
        part0 = attend_group(0, near0, near0_other, far0, (text, text_other), far0_other)
        near1_other = shift(near1, dc=1)
        far1, part0 = lax.optimization_barrier((forward(near1), part0))
        return part0, far1, near1_other, shift(far1, dc=1), text_other

    near1, far0_other = lax.optimization_barrier((near1, far0_other))
    part0, far1, near1_other, far1_other, text_other = stage(
        ready, second_stage, near1, near0, near0_other, far0, far0_other, text
    )

    text = (text, text_other)

    def third_stage(near2, near1, near1_other, far1, far1_other, text, wy, wx):
        part1 = attend_group(1, near1, near1_other, far1, text, far1_other)
        near2_other, wb, wd = shift(near2, dc=1), shift(wy, dc=1), shift(wx, dc=1)
        far2, part1 = lax.optimization_barrier((forward(near2), part1))
        return part1, near2_other, far2, shift(far2, dc=1), wb, wd

    pack3, near2, part0, wx = lax.optimization_barrier((packs[3], near2, part0, wx))
    near3 = shift(pack3, dz=4)
    part1, near2_other, far2, far2_other, wb, wd = stage(
        ready,
        third_stage,
        near2,
        near1,
        near1_other,
        far1,
        far1_other,
        text,
        wy,
        wx,
    )
    near3, near2_other = lax.optimization_barrier((near3, near2_other))
    part2 = attend_group(2, near2, near2_other, far2, text, far2_other)
    far3, far3_other, near3_other, part2 = lax.optimization_barrier(
        (forward(near3), forward(near3, flip=1), shift(near3, dc=1), part2)
    )
    part3 = attend_group(3, near3, near3_other, far3, text, far3_other)
    parts = [part0, part1, part2, part3]
    own = x % 2 * 2 + c
    order = jnp.stack([own, own ^ 1, own ^ 2, own ^ 3]).astype(jnp.int32)
    weights = [w.reshape(-1, QUARTER) for w in (wy, wb, wx, wd)]
    mixed = project(
        parts,
        order,
        weights,
        out_bias.reshape(1, D),
        out_gate.reshape(1, D),
        residual.reshape(ROWS, D),
    )
    return mixed.reshape(residual.shape)


def solution(mesh):
    placed = (
        P("fsdp", None, "seq", None),
        P("fsdp", None, "seq", None),
        P("fsdp", None, "seq", None),
        P("fsdp", "seq", None),
        P("fsdp", "seq", None),
        P("fsdp", None, "seq", None),
        P(),
        P(None, "fsdp"),
        P(),
        P("fsdp", None, "seq", None),
    )
    return jax.shard_map(
        local, mesh=mesh, in_specs=placed, out_specs=P("fsdp", None, "seq", None), check_vma=False
    )
```

```python
import functools

import jax
import jax.numpy as jnp
from jax import lax
from jax.experimental import pallas as pl
from jax.experimental.pallas import tpu as pltpu
from jax.sharding import PartitionSpec as P

HEADS = 12
HD = 128
TILE = 128
GT = 3
ROWS = GT * TILE
HID = HEADS * HD
QUARTER = HID // 4
PANEL = 192
D = 3072
TEXT = 256
GROUPS = (6, 3, 2, 1)
NEG = -1e30
SCALE = HD**-0.5 * 1.4426950408889634
AXES = ("seq", "fsdp")


def place(x, y, z, c):
    return (((x % 4) * 2 + z % 8 // 4) * 2 + c % 2) * 16 + (y % 4) * 4 + z % 4


def shift(value, dx=0, dy=0, dz=0, dc=0):
    pairs = [
        (place(x, y, z, c), place(x + dx, y + dy, z + dz, c + dc))
        for x in range(4)
        for y in range(4)
        for z in range(8)
        for c in range(2)
    ]
    return lax.ppermute(value, AXES, pairs)


def forward(value, flip=0):
    pairs = [(s, ((s + 4) % 16 if s % 4 < 2 else (s - 4) % 16) ^ flip) for s in range(16)]
    return lax.ppermute(value, "seq", pairs)


def swap(value, bit):
    return lax.ppermute(value, "seq", [(s, s ^ bit) for s in range(16)])


def across(value):
    pairs = [(s, (s - 4) % 16 if s % 4 < 2 else (s + 4) % 16) for s in range(16)]
    return lax.ppermute(value, "seq", pairs)


def join_kernel(*refs):
    first = 0
    for ref in refs[:-1]:
        refs[-1][:, first : first + ref.shape[1], :] = ref[...]
        first += ref.shape[1]


def join(*pieces):
    rows = sum(p.shape[1] for p in pieces)
    return pl.pallas_call(
        join_kernel,
        out_shape=jax.ShapeDtypeStruct((2, rows, HID), jnp.bfloat16),
        compiler_params=pltpu.CompilerParams(vmem_limit_bytes=16 * 1024 * 1024),
        cost_estimate=pl.CostEstimate(
            flops=0, bytes_accessed=8 * rows * HID, transcendentals=0
        ),
        name="join",
    )(*pieces)


def pair_kernel(k, v, out):
    out[0] = k[...]
    out[1] = v[...]


def pair(k, v, first, count, width=HD):
    rows = k.shape[0]
    return pl.pallas_call(
        pair_kernel,
        grid=(count,),
        out_shape=jax.ShapeDtypeStruct((2, rows, count * width), jnp.bfloat16),
        in_specs=[pl.BlockSpec((rows, width), lambda i: (0, first + i))] * 2,
        out_specs=pl.BlockSpec((2, rows, width), lambda i: (0, 0, i)),
        compiler_params=pltpu.CompilerParams(vmem_limit_bytes=16 * 1024 * 1024),
        cost_estimate=pl.CostEstimate(
            flops=0, bytes_accessed=8 * rows * count * width, transcendentals=0
        ),
        name="pair",
    )(k, v)


def place_kernel(where, *refs):
    for n, ref in enumerate(refs[:-1]):
        refs[-1][where[n]] = ref[...]


def place_all(where, *pieces):
    shape = (4,) + pieces[0].shape
    size = 4 * pieces[0].size
    return pl.pallas_call(
        place_kernel,
        out_shape=jax.ShapeDtypeStruct(shape, jnp.bfloat16),
        in_specs=[pl.BlockSpec(memory_space=pltpu.SMEM)]
        + [pl.BlockSpec(memory_space=pltpu.VMEM)] * 4,
        compiler_params=pltpu.CompilerParams(vmem_limit_bytes=16 * 1024 * 1024),
        cost_estimate=pl.CostEstimate(flops=0, bytes_accessed=4 * size, transcendentals=0),
        name="place",
    )(where, *pieces)


def attend_kernel(bias, q, k0, v0, a1, b0, b1, c0, c1, t0, t1, out):
    contract = (((1,), (1,)), ((), ()))
    sources = [(k0, v0)] + [(r.at[0], r.at[1]) for r in (a1, b0, b1, c0, c1)]
    for t in range(GT):
        low, high = max(0, t - 1), min(GT, t + 2)
        qt = q[t * TILE : (t + 1) * TILE, :]
        pieces = []
        peak = None
        for n, (k, _) in enumerate(sources):
            s = lax.dot_general(
                qt, k[low * TILE : high * TILE, :], contract, preferred_element_type=jnp.float32
            )
            for j in range(low, high):
                part = s[:, (j - low) * TILE : (j - low + 1) * TILE] * SCALE + bias[t, n * GT + j]
                pieces.append(part)
                peak = part if peak is None else jnp.maximum(peak, part)
        words = jnp.concatenate([t0[0], t1[0]], axis=0)
        s = lax.dot_general(qt, words, contract, preferred_element_type=jnp.float32) * SCALE
        for j in range(TEXT // TILE):
            part = s[:, j * TILE : (j + 1) * TILE]
            pieces.append(part)
            peak = jnp.maximum(peak, part)
        top = jnp.max(peak, axis=1, keepdims=True)
        total = jnp.zeros((TILE, TILE), jnp.float32)
        acc = jnp.zeros((TILE, HD), jnp.float32)
        at = 0
        for n in range(len(sources) + 1):
            if n < len(sources):
                count = high - low
                values = sources[n][1][low * TILE : high * TILE, :]
            else:
                count = TEXT // TILE
                values = jnp.concatenate([t0[1], t1[1]], axis=0)
            weights = []
            for j in range(count):
                e = jnp.exp2(pieces[at + j] - top)
                total = total + e
                weights.append(e.astype(jnp.bfloat16))
            at += count
            acc = acc + jnp.dot(
                jnp.concatenate(weights, axis=1), values, preferred_element_type=jnp.float32
            )
        row = jnp.sum(total, axis=1, keepdims=True)
        out[t * TILE : (t + 1) * TILE, :] = (acc / row).astype(jnp.bfloat16)


def attend(bias, q, k0, v0, beside, near, far, text, first, count):
    wide = pl.BlockSpec((ROWS, HD), lambda i: (0, first + i))
    words = pl.BlockSpec((2, TEXT // 2, HD), lambda i: (0, 0, first + i))
    pack = pl.BlockSpec((2, ROWS, HD), lambda i: (0, 0, i))
    whole = pl.BlockSpec((2, ROWS, HD), lambda i: (0, 0, first + i))
    units = 48 * count
    return pl.pallas_call(
        attend_kernel,
        grid=(count,),
        out_shape=jax.ShapeDtypeStruct((ROWS, count * HD), jnp.bfloat16),
        in_specs=[pl.BlockSpec(memory_space=pltpu.SMEM)]
        + [wide] * 3
        + [whole]
        + [pack] * 4
        + [words] * 2,
        out_specs=pl.BlockSpec((ROWS, HD), lambda i: (0, i)),
        compiler_params=pltpu.CompilerParams(vmem_limit_bytes=14 * 1024 * 1024),
        cost_estimate=pl.CostEstimate(
            flops=units * TILE * TILE * HD * 16,
            bytes_accessed=count * 2 * HD * (ROWS * 14 + TEXT * 2),
            transcendentals=units * TILE * TILE,
        ),
        name="attend",
    )(bias, q, k0, v0, beside, *near, *far, *text)


def project_kernel(*refs):
    parts = refs[: len(GROUPS)]
    order, wa, wb, wc, wd, bias, gate, residual, out, mine = refs[
        len(GROUPS) :
    ]
    step = pl.program_id(0)

    @pl.when(step == 0)
    def _():
        head = 0
        for part in parts:
            for n in range(part.shape[1] // HD):
                column = pl.multiple_of(order[head // 3] * QUARTER + head % 3 * HD, HD)
                mine[:, pl.ds(column, HD)] = part[:, n * HD : (n + 1) * HD]
                head += 1

    wt = jnp.concatenate([wa[...], wb[...], wc[...], wd[...]], axis=1)
    projected = lax.dot_general(
        mine[...], wt, (((1,), (1,)), ((), ())), preferred_element_type=jnp.float32
    )
    projected = (projected + bias[...]).astype(jnp.bfloat16).astype(jnp.float32)
    out[...] = (residual[...].astype(jnp.float32) + gate[...] * projected).astype(jnp.bfloat16)


def project(parts, order, weights, bias, gate, residual):
    step = 768
    panel = pl.BlockSpec((step, QUARTER), lambda i: (i, 0))
    return pl.pallas_call(
        project_kernel,
        grid=(D // step,),
        out_shape=jax.ShapeDtypeStruct((ROWS, D), jnp.bfloat16),
        in_specs=[pl.BlockSpec(part.shape, lambda i: (0, 0)) for part in parts]
        + [pl.BlockSpec(memory_space=pltpu.SMEM)]
        + [panel] * 4
        + [
            pl.BlockSpec((1, step), lambda i: (0, i)),
            pl.BlockSpec((1, step), lambda i: (0, i)),
            pl.BlockSpec((ROWS, step), lambda i: (0, i)),
        ],
        out_specs=pl.BlockSpec((ROWS, step), lambda i: (0, i)),
        scratch_shapes=[
            pltpu.VMEM((ROWS, HID), jnp.bfloat16),
        ],
        compiler_params=pltpu.CompilerParams(vmem_limit_bytes=24 * 1024 * 1024),
        cost_estimate=pl.CostEstimate(
            flops=2 * ROWS * HID * D,
            bytes_accessed=2 * D * HID + 4 * ROWS * D,
            transcendentals=0,
        ),
        name="project",
    )(*parts, order, *weights, bias, gate, residual)


def stage(ready, work, *operands):
    shapes = jax.eval_shape(work, *operands)
    return lax.cond(
        ready,
        work,
        lambda *_: tuple(jnp.zeros(s.shape, s.dtype) for s in shapes),
        *operands,
    )


def local(
    queries,
    key_rows,
    value_rows,
    text_keys,
    text_values,
    residual,
    out_gate,
    out_weight,
    out_bias,
    tile_lists,
):
    seq, fsdp = lax.axis_index("seq"), lax.axis_index("fsdp")
    x, zh, c = seq // 4, seq // 2 % 2, seq % 2
    y, zl = fsdp // 4, fsdp % 4
    q = queries.reshape(ROWS, HID)
    k0, v0 = key_rows.reshape(ROWS, HID), value_rows.reshape(ROWS, HID)

    far_spot = jnp.where(zh == 0, seq - 2, seq + 2)
    spots = jnp.stack(
        [seq, seq ^ 1, seq ^ 2, seq ^ 3, far_spot, far_spot ^ 1]
    )
    inside = (spots >= 0) & (spots < 16)
    candidates = spots[:, None] + 16 * jnp.arange(GT, dtype=jnp.int32)[None, :]
    listed = tile_lists[0, :, 0, :]
    present = jnp.any(listed[:, None, None, :] == candidates[None, :, :, None], axis=3)
    present = present & inside[None, :, None]
    bias = jnp.where(present, 0.0, NEG).astype(jnp.float32).reshape(GT, 6 * GT)

    steps = jnp.array([0, 1, -1, 2], jnp.int32)
    firsts = [sum(GROUPS[:g]) for g in range(len(GROUPS))]
    packs = [pair(k0, v0, first, count) for first, count in zip(firsts, GROUPS)]

    def attend_group(g, near, near_other, far, text, far_other):
        return attend(
            bias,
            q,
            k0,
            v0,
            beside,
            (near, near_other),
            (far, far_other),
            text,
            firsts[g],
            GROUPS[g],
        )

    text = pair(text_keys[0], text_values[0], 0, 1, HID)
    piece = lax.dynamic_slice(
        out_weight.T, (0, (x % 2 * 2 + c) * QUARTER), (PANEL, QUARTER)
    )
    text_z = swap(text, 2)
    own = pair(k0, v0, 0, HEADS)
    pack0, own, wz1, wz2, wz3, text_z = lax.optimization_barrier(
        (
            packs[0],
            own,
            shift(piece, dz=1),
            shift(piece, dz=-1),
            shift(piece, dz=2),
            text_z,
        )
    )
    packs, bias, beside, wz1, wz2, wz3 = lax.optimization_barrier(
        (
            packs[1:],
            bias,
            shift(own, dc=1),
            wz1,
            wz2,
            wz3,
        )
    )
    near0 = shift(pack0, dz=4)
    packs = (pack0,) + tuple(packs)
    ready = tile_lists[0, 0, 0, 0] > -2

    def weight_stage(piece, wz1, wz2, wz3, text, text_z):
        wz = place_all((zl - steps) % 4, piece, wz1, wz2, wz3)
        wy1, text = lax.optimization_barrier((shift(wz, dy=1), join(text, text_z)))
        wy = place_all((y - steps) % 4, wz, wy1, shift(wz, dy=-1), shift(wz, dy=2))
        text = join(text, swap(text, 4))
        text = join(text, swap(text, 8))
        return wy.reshape(D, QUARTER), text

    wy, text = stage(ready, weight_stage, piece, wz1, wz2, wz3, text, text_z)
    pack1, wy = lax.optimization_barrier((packs[1], wy))
    near1 = shift(pack1, dz=4)
    near0, wy = lax.optimization_barrier((near0, wy))
    wx = across(wy)

    def first_stage(near0, text):
        near0_other = shift(near0, dc=1)
        far0, text = lax.optimization_barrier((forward(near0), swap(text, 1)))
        return far0, near0_other, shift(far0, dc=1), text

    far0, near0_other, far0_other, text_other = stage(ready, first_stage, near0, text)
    text = (text, text_other)

    def second_stage(near1, near0, near0_other, far0, far0_other, text):
        part0 = attend_group(0, near0, near0_other, far0, text, far0_other)
        near1_other = shift(near1, dc=1)
        far1, part0 = lax.optimization_barrier((forward(near1), part0))
        return part0, far1, near1_other, shift(far1, dc=1)

    pack2, near1, far0_other = lax.optimization_barrier((packs[2], near1, far0_other))
    near2 = shift(pack2, dz=4)
    part0, far1, near1_other, far1_other = stage(
        ready, second_stage, near1, near0, near0_other, far0, far0_other, text
    )

    def third_stage(near2, near1, near1_other, far1, far1_other, text, wy, wx):
        part1 = attend_group(1, near1, near1_other, far1, text, far1_other)
        near2_other, wb, wd = shift(near2, dc=1), shift(wy, dc=1), shift(wx, dc=1)
        far2, part1 = lax.optimization_barrier((forward(near2), part1))
        return part1, near2_other, far2, shift(far2, dc=1), wb, wd

    pack3, near2, part0, wx = lax.optimization_barrier((packs[3], near2, part0, wx))
    near3 = shift(pack3, dz=4)
    part1, near2_other, far2, far2_other, wb, wd = stage(
        ready,
        third_stage,
        near2,
        near1,
        near1_other,
        far1,
        far1_other,
        text,
        wy,
        wx,
    )
    near3, near2_other = lax.optimization_barrier((near3, near2_other))
    part2 = attend_group(2, near2, near2_other, far2, text, far2_other)
    far3, far3_other, near3_other, part2 = lax.optimization_barrier(
        (forward(near3), forward(near3, flip=1), shift(near3, dc=1), part2)
    )
    part3 = attend_group(3, near3, near3_other, far3, text, far3_other)
    parts = [part0, part1, part2, part3]
    own = x % 2 * 2 + c
    order = jnp.stack([own, own ^ 1, own ^ 2, own ^ 3]).astype(jnp.int32)
    weights = [w.reshape(-1, QUARTER) for w in (wy, wb, wx, wd)]
    mixed = project(
        parts,
        order,
        weights,
        out_bias.reshape(1, D),
        out_gate.reshape(1, D),
        residual.reshape(ROWS, D),
    )
    return mixed.reshape(residual.shape)


def solution(mesh):
    placed = (
        P("fsdp", None, "seq", None),
        P("fsdp", None, "seq", None),
        P("fsdp", None, "seq", None),
        P("fsdp", "seq", None),
        P("fsdp", "seq", None),
        P("fsdp", None, "seq", None),
        P(),
        P(None, "fsdp"),
        P(),
        P("fsdp", None, "seq", None),
    )
    return jax.shard_map(
        local, mesh=mesh, in_specs=placed, out_specs=P("fsdp", None, "seq", None), check_vma=False
    )
```
